128 devices in a mesh: space: 32 (over y, z_hi, x), head: 4 (over z_lo, core).
Axes of the slice: x: 4, y: 4, z: 4 (z_hi: 2, z_lo: 2; z = z_hi * 2 + z_lo), core: 2. Of those that a mesh axis runs over, the one named last changes fastest.
Arguments:
- levels: bfloat16 [13, 192, 48, 512], P(None, 'space'), may hold values from -6 to 6
- latent_query: bfloat16 [3, 512], replicated, may hold values from -200 to 200
- w_pq: bfloat16 [512, 512], P(None, 'head'), may hold values from -0.25 to 0.25
- w_pk: bfloat16 [512, 512], P(None, 'head'), may hold values from -0.25 to 0.25
- w_pv: bfloat16 [512, 512], P(None, 'head'), may hold values from -0.25 to 0.25
- w_po: bfloat16 [512, 512], P('head'), may hold values from -0.25 to 0.25
- layer_norm_gain: float32 [512], replicated, may hold values from 0.5 to 6
- window_query_weight: bfloat16 [512, 512], P(None, 'head'), may hold values from -0.25 to 0.25
- window_key_weight: bfloat16 [512, 512], P(None, 'head'), may hold values from -0.25 to 0.25
- window_value_weight: bfloat16 [512, 512], P(None, 'head'), may hold values from -0.25 to 0.25
- window_output_weight: bfloat16 [512, 512], P('head'), may hold values from -0.25 to 0.25
- cotangent: bfloat16 [3, 192, 48, 512], P(None, 'space'), may hold values from -6 to 6
Outputs:
- grad_levels: bfloat16 [13, 192, 48, 512], P(None, 'space', None, 'head')
The draws below stay inside these ranges and needn't reach their ends.
All inputs are finite; a program needn't handle non-finite values.
Results may differ from the reference program's by a relative error of at most 0.034.
The reference program's roundings to bfloat16 on the way count: a program that leaves them out, or rounds other values in their place, can miss the bound.
Values may be sent and summed in bfloat16 or wider, within the bound.
A program may use at most 64 MiB of HBM per device.

```python
import jax
import jax.numpy as jnp
from jax import lax

MODEL_DIMENSION = 512
HEADS = 16
HEAD_DIM = 32
LEVELS = 13
LATENT = 3
WIN_LAT = 6
WIN_LON = 12
LON = 48
LAT = 192


def draw_latent_query(key, part):
    key = jax.random.fold_in(key, 11)
    base = jax.random.normal(key, (LATENT, MODEL_DIMENSION), jnp.float32)
    return jnp.clip(base, -4.0, 4.0).astype(jnp.bfloat16)


def draw_layer_norm_gain(key, part):
    key = jax.random.fold_in(key, 12)
    return jax.random.uniform(key, (MODEL_DIMENSION,), jnp.float32, 0.5, 1.5)


def block_scale(rng, dims, split, least, top_value):
    def one(dim, parts):
        steps = jax.random.uniform(jax.random.fold_in(jax.random.fold_in(rng, 6), dim), (parts,), jnp.float32, least / len(split), top_value / len(split))
        return jnp.repeat(jnp.exp(steps), dims[dim] // parts).reshape((-1,) + (1,) * (len(dims) - dim - 1))

    level = one(*split[0])
    for cut in split[1:]:
        level = level * one(*cut)
    return level


def scatter_about(rng, dims, scale, bound, pieces=(), kind=jnp.bfloat16):
    gain = block_scale(rng, dims, pieces, -0.22, 0.18) if pieces else 1.0
    drawn = jax.random.normal(rng, dims, jnp.float32) * scale * gain
    return jnp.minimum(jnp.maximum(drawn, -bound), bound).astype(kind)


def setup_inputs(seed: int = 0) -> dict:
    key_of = jax.random.split(jax.random.key(seed), 13)
    return {
        "levels": scatter_about(key_of[0], (LEVELS, LAT, LON, MODEL_DIMENSION), 1.0, 6.0, ((1, 32),)),
        "latent_query": draw_latent_query(jax.random.fold_in(key_of[12], 71), 0),
        "w_pq": scatter_about(key_of[2], (MODEL_DIMENSION, MODEL_DIMENSION), MODEL_DIMENSION ** -0.5, 0.25, ((1, 4),)),
        "w_pk": scatter_about(key_of[3], (MODEL_DIMENSION, MODEL_DIMENSION), MODEL_DIMENSION ** -0.5, 0.25, ((1, 4),)),
        "w_pv": scatter_about(key_of[4], (MODEL_DIMENSION, MODEL_DIMENSION), MODEL_DIMENSION ** -0.5, 0.25, ((1, 4),)),
        "w_po": scatter_about(key_of[5], (MODEL_DIMENSION, MODEL_DIMENSION), MODEL_DIMENSION ** -0.5, 0.25, ((0, 4),)),
        "layer_norm_gain": draw_layer_norm_gain(jax.random.fold_in(key_of[12], 71), 0),
        "window_query_weight": scatter_about(key_of[7], (MODEL_DIMENSION, MODEL_DIMENSION), MODEL_DIMENSION ** -0.5, 0.25, ((1, 4),)),
        "window_key_weight": scatter_about(key_of[8], (MODEL_DIMENSION, MODEL_DIMENSION), MODEL_DIMENSION ** -0.5, 0.25, ((1, 4),)),
        "window_value_weight": scatter_about(key_of[9], (MODEL_DIMENSION, MODEL_DIMENSION), MODEL_DIMENSION ** -0.5, 0.25, ((1, 4),)),
        "window_output_weight": scatter_about(key_of[10], (MODEL_DIMENSION, MODEL_DIMENSION), MODEL_DIMENSION ** -0.5, 0.25, ((0, 4),)),
        "cotangent": scatter_about(key_of[11], (LATENT, LAT, LON, MODEL_DIMENSION), 1.0, 6.0, ((1, 32),)),
    }


def to_windows(grid):
    level_depth, lat_rows, lon_cells, feature = grid.shape
    blocks = grid.reshape(level_depth, lat_rows // WIN_LAT, WIN_LAT, lon_cells // WIN_LON, WIN_LON, feature)
    blocks = blocks.transpose(1, 3, 0, 2, 4, 5)
    return blocks.reshape(lat_rows // WIN_LAT * (lon_cells // WIN_LON), level_depth * WIN_LAT * WIN_LON, feature)

def from_windows(windows, level_depth, lat_rows, lon_cells):
    feature = windows.shape[-1]
    blocks = windows.reshape(lat_rows // WIN_LAT, lon_cells // WIN_LON, level_depth, WIN_LAT, WIN_LON, feature)
    return blocks.transpose(2, 0, 3, 1, 4, 5).reshape(level_depth, lat_rows, lon_cells, feature)

def window_grads(queries, keys_in, values_in, grad_out, at_edge):
    window_count, window_len, feature = queries.shape
    head_count = feature // HEAD_DIM
    shape_heads = (window_count, window_len, head_count, HEAD_DIM)
    score_scale = HEAD_DIM ** (-0.5)
    q_heads = queries.reshape(shape_heads).astype(jnp.float32)
    k_heads = keys_in.reshape(shape_heads).astype(jnp.float32)
    v_heads = values_in.reshape(shape_heads).astype(jnp.float32)
    o_heads = grad_out.reshape(shape_heads).astype(jnp.float32)
    scores = jnp.einsum('wqhe,wkhe->whqk', q_heads, k_heads) * score_scale
    row_in = jnp.arange(window_len) // WIN_LON % WIN_LAT
    upper = row_in < WIN_LAT // 2
    same_part = upper[:, None] == upper[None, :]
    allowed = jnp.logical_or(same_part[None, None], jnp.logical_not(at_edge)[:, None, None, None])
    scores = jnp.where(allowed, scores, -1e+30)
    prob_f = jax.nn.softmax(scores, axis=-1)
    prob_b = prob_f.astype(jnp.bfloat16)
    grad_v = jnp.einsum('whqk,wqhe->wkhe', prob_b.astype(jnp.float32), o_heads).astype(jnp.bfloat16)
    window_dp = jnp.einsum('wqhe,wkhe->whqk', o_heads, v_heads)
    window_ds = (prob_f * (window_dp - lax.optimization_barrier(jnp.sum(prob_f * window_dp, axis=-1, keepdims=True))) * score_scale).astype(jnp.bfloat16)
    ds_float = window_ds.astype(jnp.float32)
    grad_q = jnp.einsum('whqk,wkhe->wqhe', ds_float, k_heads).astype(jnp.bfloat16)
    grad_k = jnp.einsum('whqk,wqhe->wkhe', ds_float, q_heads).astype(jnp.bfloat16)
    return (grad_q.reshape(window_count, window_len, feature), grad_k.reshape(window_count, window_len, feature), grad_v.reshape(window_count, window_len, feature))

def reference(levels, latent_query, w_pq, w_pk, w_pv, w_po, layer_norm_gain, window_query_weight, window_key_weight, window_value_weight, window_output_weight, cotangent):
    brain_float = jnp.bfloat16
    single_float = jnp.float32
    score_scale = HEAD_DIM ** (-0.5)
    patches = LAT * LON
    level_flat = levels.reshape(LEVELS * patches, MODEL_DIMENSION)
    query_proj = jnp.dot(latent_query, w_pq, preferred_element_type=single_float).astype(brain_float)
    query_heads = query_proj.reshape(LATENT, HEADS, HEAD_DIM).astype(single_float)
    key_proj = jnp.dot(level_flat, w_pk, preferred_element_type=single_float).astype(brain_float).reshape(LEVELS, patches, HEADS, HEAD_DIM)
    value_proj = jnp.dot(level_flat, w_pv, preferred_element_type=single_float).astype(brain_float).reshape(LEVELS, patches, HEADS, HEAD_DIM)
    level_scores = jnp.einsum('ahe,lphe->ahlp', query_heads, key_proj.astype(single_float)) * score_scale
    level_prob = jax.nn.softmax(level_scores, axis=2)
    level_prob_b = level_prob.astype(brain_float)
    mixed = jnp.einsum('ahlp,lphe->aphe', level_prob_b.astype(single_float), value_proj.astype(single_float)).astype(brain_float)
    mixed_flat = mixed.reshape(LATENT * patches, MODEL_DIMENSION)
    projected = jnp.dot(mixed_flat, w_po, preferred_element_type=single_float).reshape(LATENT, patches, MODEL_DIMENSION)
    latent = (latent_query.astype(single_float)[:, None, :] + projected).astype(brain_float).reshape(LATENT, LAT, LON, MODEL_DIMENSION)
    half_lat = WIN_LAT // 2
    half_lon = WIN_LON // 2
    rolled_input = jnp.roll(latent, (-half_lat, -half_lon), axis=(1, 2))
    shifted_cotangent = jnp.roll(cotangent, (-half_lat, -half_lon), axis=(1, 2))
    z_float = rolled_input.astype(single_float)
    centered_input = z_float - lax.optimization_barrier(jnp.mean(z_float, axis=-1, keepdims=True))
    inverse_deviation = lax.rsqrt(lax.optimization_barrier(jnp.mean(centered_input * centered_input, axis=-1, keepdims=True)) + 1e-05)
    standardized_input = centered_input * inverse_deviation
    normalized_input = (standardized_input * layer_norm_gain.astype(single_float)).astype(brain_float).reshape(-1, MODEL_DIMENSION)
    grid_dimensions = (LATENT, LAT, LON, MODEL_DIMENSION)
    win_q = jnp.dot(normalized_input, window_query_weight, preferred_element_type=single_float).astype(brain_float).reshape(grid_dimensions)
    win_k = jnp.dot(normalized_input, window_key_weight, preferred_element_type=single_float).astype(brain_float).reshape(grid_dimensions)
    win_v = jnp.dot(normalized_input, window_value_weight, preferred_element_type=single_float).astype(brain_float).reshape(grid_dimensions)
    out_grad = jnp.dot(shifted_cotangent.reshape(-1, MODEL_DIMENSION), window_output_weight.T, preferred_element_type=single_float).astype(brain_float).reshape(grid_dimensions)
    lat_wins = LAT // WIN_LAT
    lon_wins = LON // WIN_LON

    def split_windows(grid):
        return to_windows(grid).reshape(lat_wins, lon_wins, -1, MODEL_DIMENSION)
    last_rows = jnp.arange(lat_wins) == lat_wins - 1

    def window_step(operands):
        return window_grads(operands[0], operands[1], operands[2], operands[3], jnp.full((lon_wins,), operands[4]))
    grads = lax.map(window_step, (split_windows(win_q), split_windows(win_k), split_windows(win_v), split_windows(out_grad), last_rows))
    grid_grads = [from_windows(part.reshape(lat_wins * lon_wins, -1, MODEL_DIMENSION), LATENT, LAT, LON).reshape(-1, MODEL_DIMENSION) for part in grads]
    normed_gradient = jnp.dot(grid_grads[0], window_query_weight.T, preferred_element_type=single_float)
    normed_gradient = normed_gradient + jnp.dot(grid_grads[1], window_key_weight.T, preferred_element_type=single_float)
    normed_gradient = normed_gradient + jnp.dot(grid_grads[2], window_value_weight.T, preferred_element_type=single_float)
    standardized_gradient = normed_gradient.reshape(grid_dimensions) * layer_norm_gain.astype(single_float)
    shift_gradient = inverse_deviation * (standardized_gradient - lax.optimization_barrier(jnp.mean(standardized_gradient, axis=-1, keepdims=True)) - standardized_input * lax.optimization_barrier(jnp.mean(standardized_gradient * standardized_input, axis=-1, keepdims=True)))
    branch = jnp.roll(shift_gradient, (half_lat, half_lon), axis=(1, 2))
    latent_grad = (cotangent.astype(single_float) + branch).astype(brain_float)
    d_mixed = jnp.dot(latent_grad.reshape(-1, MODEL_DIMENSION), w_po.T, preferred_element_type=single_float).astype(brain_float)
    d_mixed = d_mixed.reshape(LATENT, patches, HEADS, HEAD_DIM).astype(single_float)
    grad_value = jnp.einsum('ahlp,aphe->lphe', level_prob_b.astype(single_float), d_mixed).astype(brain_float)
    level_dp = jnp.einsum('aphe,lphe->ahlp', d_mixed, value_proj.astype(single_float))
    level_ds = level_prob * (level_dp - lax.optimization_barrier(jnp.sum(level_prob * level_dp, axis=2, keepdims=True))) * score_scale
    grad_key = jnp.einsum('ahlp,ahe->lphe', level_ds, query_heads).astype(brain_float)
    total = jnp.dot(grad_key.reshape(-1, MODEL_DIMENSION), w_pk.T, preferred_element_type=single_float)
    total = total + jnp.dot(grad_value.reshape(-1, MODEL_DIMENSION), w_pv.T, preferred_element_type=single_float)
    return total.astype(brain_float).reshape(LEVELS, LAT, LON, MODEL_DIMENSION)
```

```python
import functools

import jax
import jax.numpy as jnp
from jax import lax
from jax.experimental import pallas as pl
from jax.experimental.pallas import tpu as pltpu
from jax.sharding import PartitionSpec as P

X_CHIPS = 4
LEVELS = 13
CHUNKS = 7
WIDTH = 512
PATCH = 72
HALF = 108
SCALE = 32 ** (-0.5)
MESH = pl.DeviceIdType.MESH
BF = jnp.bfloat16
F32 = jnp.float32
PK, PV, PO, WO, WQ, WK, WV = range(7)
BY_COLUMN = (True, True, False, False, True, True, True)


def nn(left, right):
    return jnp.dot(left, right, preferred_element_type=F32)


def nt(left, right):
    return lax.dot_general(left, right, (((1,), (1,)), ((), ())), preferred_element_type=F32)


def rows(n):
    return lax.broadcasted_iota(jnp.int32, (n, 1), 0)


def cols(n):
    return lax.broadcasted_iota(jnp.int32, (1, n), 1)


def hot(condition):
    return jnp.where(condition, 1.0, 0.0).astype(BF)


def kernel(
    levels, lq_ref, wpq_ref, wpk, wpv, wpo, gain_ref, wq, wk, wv, wo, cot,
    out,
    lev, cotx, full, lqs, qbuf, qbt, ea, ead, sw, sp, pm, bias,
    xs, vs, ps, dps, cot_l, cot_win, lat_l, lat_in, ds_l, ds_in,
    win_q, win_k, win_v, win_o, g_q, g_k, g_v, zs, inv_s, ob, rv, fin,
    loc_sem, w_send, w_recv, q_send, q_recv, e_send, e_recv, a_send, a_recv, own_sem, out_sem,
):
    s = lax.axis_index("space")
    n = lax.axis_size("space")
    h = lax.axis_index("head")
    sib = h + 1 - 2 * lax.rem(h, 2)
    over = lax.rem(h + 2, 4)
    diag = 3 - h
    z_other = s + X_CHIPS - 2 * X_CHIPS * lax.rem(lax.div(s, X_CHIPS), 2)
    prev = lax.rem(s + n - 1, n)
    after = lax.rem(s + 1, n)
    weights = (wpk, wpv, wpo, wo, wq, wk, wv)

    def region(k, head, part):
        if BY_COLUMN[k]:
            along = slice(None) if part is None else pl.ds(256 * part, 256)
            return full.at[k, along, pl.ds(pl.multiple_of(head * 128, 128), 128)]
        if part is None:
            return full.at[k, pl.ds(pl.multiple_of(head * 128, 128), 128)]
        return full.at[k, pl.ds(pl.multiple_of(head * 128 + 64 * part, 64), 64)]

    def shard(k, part):
        if part is None:
            return weights[k]
        size = 256 if BY_COLUMN[k] else 64
        return weights[k].at[pl.ds(size * part, size)]

    def remote(src, dst, send, recv, device):
        return pltpu.make_async_remote_copy(
            src_ref=src, dst_ref=dst, send_sem=send, recv_sem=recv,
            device_id=device, device_id_type=MESH,
        )

    b0 = lax.div(12 * h + 6, 16)
    b1 = lax.rem(b0 + 1, 3)
    base = 12 * h + 6 - 16 * b0
    local = []
    for block, where in ((b0, 0), (b1, 16)):
        at = pl.ds(pl.multiple_of(16 * block, 16), 16)
        local.append((levels.at[:, :, at, :], lev.at[pl.ds(0, LEVELS), :, pl.ds(where, 16), :]))
        local.append((cot.at[:, :, at, :], cotx.at[:, :, pl.ds(where, 16), :]))
    for k in range(7):
        local.append((weights[k], region(k, h, None)))
    local = [
        pltpu.make_async_copy(src, dst, loc_sem.at[i]) for i, (src, dst) in enumerate(local)
    ]
    for copy in local:
        copy.start()

    barrier = pltpu.get_barrier_semaphore()
    for device in ((s, sib), (s, over), (s, diag), (z_other, over), (prev, h), (after, h)):
        pl.semaphore_signal(barrier, inc=1, device_id=device, device_id_type=MESH)
    pl.semaphore_wait(barrier, 6)

    sent = []

    def send(copy):
        copy.start()
        sent.append(copy)

    for k in range(7):
        send(remote(shard(k, 0), region(k, h, 0), w_send.at[k, 1], w_recv.at[k, 1], (s, over)))
        send(remote(shard(k, 1), region(k, h, 1), w_send.at[k, 2], w_recv.at[k, 2], (z_other, over)))
        send(remote(shard(k, None), region(k, h, None), w_send.at[k, 0], w_recv.at[k, 0], (s, sib)))

    lqs[...] = jnp.zeros_like(lqs)
    lqs[0:3, :] = lq_ref[...].astype(F32)
    lq16 = lqs[...].astype(BF)
    qbuf[h] = nn(lq16, wpq_ref[...]).astype(BF)
    for r, peer in enumerate((sib, over, diag)):
        send(remote(qbuf.at[h], qbuf.at[h], q_send.at[r], q_recv.at[r], (s, peer)))

    def wait_in(k, i, head, part, peer):
        remote(region(k, head, part), region(k, head, part), w_send.at[k, i], w_recv.at[k, i], (s, peer)).wait_recv()

    def relay(k):
        for part in range(2):
            wait_in(k, 1 + part, over, part, over)
            piece = region(k, over, part)
            send(remote(piece, piece, w_send.at[k, 3 + part], w_recv.at[k, 3 + part], (s, sib)))

    def have(k):
        local[4 + k].wait()
        wait_in(k, 0, sib, None, sib)
        for part in range(2):
            wait_in(k, 3 + part, diag, part, sib)

    lane_head = lax.div(cols(WIDTH), 32)
    for a in range(3):
        ea[a] = hot(rows(128) == a * 16 + lane_head)
        ead[a] = hot(lax.rem(rows(128), 64) == a * 16 + lane_head)
    w_row = lax.rem(rows(256), 128)
    w_a = lax.div(w_row, 36)
    w_k = lax.rem(w_row, 36)
    upper = rows(256) < 128
    w_patch = w_a * 72 + w_k + jnp.where(upper, 36, 0)
    w_col = jnp.where(w_row < HALF, w_patch, -1)
    sw[...] = hot(w_col == cols(224))
    p_a = lax.div(rows(224), 72)
    p_k = lax.rem(rows(224), 72)
    p_col = p_a * 36 + jnp.where(p_k >= 36, p_k - 36, 128 + p_k)
    sp[...] = hot(jnp.where(p_a < 3, p_col, -1) == cols(256))
    o_row = lax.div(rows(288), 48)
    o_lon = lax.rem(lax.rem(rows(288), 48) + 42, 48)
    o_col = lax.div(o_lon, 12) * 72 + o_row * 12 + lax.rem(o_lon, 12)
    pm[...] = hot(o_col == cols(288))
    pad_key = lax.rem(rows(256), 128) >= HALF
    crossing = jnp.logical_and((rows(256) < 128) != (cols(256) < 128), s == n - 1)
    bias[...] = jnp.where(jnp.logical_or(pad_key, crossing), -1e30, 0.0).astype(F32)
    lq_row = nn(hot(jnp.where(w_row < HALF, w_a, -1) == cols(16)), lq16)

    local[0].wait()
    local[2].wait()
    lev[LEVELS] = jnp.zeros((6, 32, WIDTH), BF)
    in_row = lax.div(rows(PATCH), 12)
    take = hot(in_row * 32 + base + lax.rem(rows(PATCH), 12) == cols(192))

    def pick(c, carry):
        two = [nn(take, lev[2 * c + i].reshape(192, WIDTH)) for i in range(2)]
        xs[c] = jnp.concatenate(two, axis=0).astype(BF)
        return carry

    lax.fori_loop(0, CHUNKS, pick, 0)

    local[1].wait()
    local[3].wait()
    h_row = rows(128)
    h_a = jnp.where(h_row < HALF, lax.div(h_row, 36), -1)
    h_k = lax.rem(h_row, 36)
    h_at = lax.div(h_k, 12) * 32 + base + lax.rem(h_k, 12)
    for half, keep in ((0, cot_l), (1, None)):
        total = None
        for a in range(3):
            spot = jnp.where(h_a == a, h_at + half * 96, -1)
            term = nn(hot(spot == cols(192)), cotx[a].reshape(192, WIDTH))
            total = term if total is None else total + term
        if half == 0:
            cot_l[...] = total.astype(BF)
            send(remote(cot_l, cot_win.at[pl.ds(128, 128)], e_send.at[0], e_recv.at[0], (prev, h)))
        else:
            cot_win[0:128] = total.astype(BF)

    for r, peer in enumerate((sib, over, diag)):
        remote(qbuf.at[peer], qbuf.at[peer], q_send.at[r], q_recv.at[r], (s, peer)).wait_recv()
    q16 = jnp.concatenate([qbuf[i] for i in range(4)], axis=1)
    q_rows = nn(hot(lax.div(lax.rem(rows(128), 64), 16) == cols(16)), q16)
    qbt[...] = jnp.where(lax.rem(rows(128), 16) == lane_head, q_rows, 0.0).astype(BF)
    relay(PK)
    relay(PV)
    have(PK)
    have(PV)

    def project(c, carry):
        x = xs[c]
        key = nn(x, full[PK]).astype(BF)
        ps[c] = nt(key, qbt[...]) * SCALE
        vs[c] = nn(x, full[PV]).astype(BF)
        return carry

    lax.fori_loop(0, CHUNKS, project, 0)
    relay(PO)

    def level(ref, l):
        return ref[l // 2, (l % 2) * PATCH:(l % 2 + 1) * PATCH]

    top = level(ps, 0)
    for l in range(1, LEVELS):
        top = jnp.maximum(top, level(ps, l))
    norm = jnp.zeros_like(top)
    for l in range(LEVELS):
        e = jnp.exp(level(ps, l) - top)
        ps[l // 2, (l % 2) * PATCH:(l % 2 + 1) * PATCH] = e
        norm = norm + e
    inverse = 1.0 / norm
    for l in range(LEVELS):
        ps[l // 2, (l % 2) * PATCH:(l % 2 + 1) * PATCH] = level(ps, l) * inverse
    ps[CHUNKS - 1, PATCH:] = jnp.zeros((PATCH, 128), F32)

    def mix(c, total):
        value = vs[c].astype(F32)
        prob = ps[c].astype(BF)
        new = []
        for a in range(3):
            both = nn(prob, ea[a]) * value
            new.append(total[a] + both[:PATCH] + both[PATCH:])
        return tuple(new)

    mixed = lax.fori_loop(0, CHUNKS, mix, tuple(jnp.zeros((PATCH, WIDTH), F32) for _ in range(3)))
    mixed = jnp.concatenate(list(mixed) + [jnp.zeros((8, WIDTH), F32)], axis=0).astype(BF)
    mixed = nn(sw[...], mixed).astype(BF)
    have(PO)
    latent = (lq_row + nn(mixed, full[PO])).astype(BF)
    lat_l[...] = latent[128:]
    send(remote(lat_l, lat_in, e_send.at[1], e_recv.at[1], (prev, h)))

    relay(WO)
    relay(WQ)
    have(WO)
    remote(cot_l, cot_win.at[pl.ds(128, 128)], e_send.at[0], e_recv.at[0], (prev, h)).wait_recv()
    win_o[...] = nt(cot_win[...], full[WO]).astype(BF)
    relay(WK)
    relay(WV)
    remote(lat_l, lat_in, e_send.at[1], e_recv.at[1], (prev, h)).wait_recv()
    z = jnp.concatenate([latent[:128], lat_in[...]], axis=0).astype(F32)
    z = z - jnp.mean(z, axis=-1, keepdims=True)
    inv = lax.rsqrt(jnp.mean(z * z, axis=-1, keepdims=True) + 1e-05)
    z = z * inv
    zs[...] = z
    inv_s[...] = jnp.broadcast_to(inv, (256, 128))
    normed = (z * gain_ref[...]).astype(BF)
    have(WQ)
    win_q[...] = nn(normed, full[WQ]).astype(BF)
    have(WK)
    win_k[...] = nn(normed, full[WK]).astype(BF)
    have(WV)
    win_v[...] = nn(normed, full[WV]).astype(BF)

    def attend(g, carry):
        lanes = pl.ds(pl.multiple_of(g * 128, 128), 128)
        qg, kg, vg, og = win_q[:, lanes], win_k[:, lanes], win_v[:, lanes], win_o[:, lanes]
        kt = kg.astype(F32).T.astype(BF)
        gk = jnp.zeros((256, 128), F32)
        gv = jnp.zeros((256, 128), F32)
        gq = []
        for i in range(4):
            mine = hot(lax.div(cols(128), 32) == i)
            qm = qg * mine
            om = og * mine
            score = nt(kg, qm) * SCALE + bias[...]
            e = jnp.exp(score - jnp.max(score, axis=0, keepdims=True))
            prob = e * (1.0 / jnp.sum(e, axis=0, keepdims=True))
            gv = gv + nn(prob.astype(BF), om)
            dp = nt(vg, om)
            dp = dp - jnp.sum(prob * dp, axis=0, keepdims=True)
            ds = (prob * dp * SCALE).astype(BF)
            gk = gk + nn(ds, qm)
            gq.append(nn(kt[32 * i:32 * i + 32], ds))
        g_k[:, lanes] = gk.astype(BF)
        g_v[:, lanes] = gv.astype(BF)
        g_q[:, lanes] = jnp.concatenate(gq, axis=0).T.astype(BF)
        return carry

    lax.fori_loop(0, 4, attend, 0)
    d = nt(g_q[...], full[WQ]) + nt(g_k[...], full[WK]) + nt(g_v[...], full[WV])
    d = d * gain_ref[...]
    z = zs[...]
    d = inv_s[:, 0:1] * (
        d - jnp.mean(d, axis=-1, keepdims=True) - z * jnp.mean(d * z, axis=-1, keepdims=True)
    )
    ds_l[...] = d[128:].astype(BF)
    send(remote(ds_l, ds_in, e_send.at[2], e_recv.at[2], (after, h)))
    grad_u = (cot_win[0:128].astype(F32) + d[:128]).astype(BF)
    remote(ds_l, ds_in, e_send.at[2], e_recv.at[2], (after, h)).wait_recv()
    grad_l = (cot_l[...].astype(F32) + ds_in[...].astype(F32)).astype(BF)
    grad = jnp.concatenate([grad_u, grad_l], axis=0)
    d_mixed = nt(grad, full[PO]).astype(BF)
    d_mixed = nn(sp[...], d_mixed)
    d_mixed = [d_mixed[PATCH * a:PATCH * (a + 1)] for a in range(3)]

    def level_dp(c, carry):
        value = vs[c].astype(F32)
        total = jnp.zeros((2 * PATCH, 128), F32)
        for a in range(3):
            prod = jnp.concatenate([d_mixed[a] * value[:PATCH], d_mixed[a] * value[PATCH:]], axis=0)
            high = prod.astype(BF)
            low = (prod - high.astype(F32)).astype(BF)
            total = total + nt(high, ead[a]) + nt(low, ead[a])
        dps[c] = total
        return carry

    lax.fori_loop(0, CHUNKS, level_dp, 0)
    mean = jnp.zeros((PATCH, 128), F32)
    for l in range(LEVELS):
        mean = mean + level(ps, l) * level(dps, l)
    low_lanes = cols(128) < 64

    def finish(c, carry):
        prob = ps[c]
        dp = dps[c]
        ds = prob * jnp.concatenate([dp[:PATCH] - mean, dp[PATCH:] - mean], axis=0) * SCALE
        high = ds.astype(BF).astype(F32)
        ds = jnp.where(low_lanes, high, ds - high).astype(BF)
        grad_key = nn(ds, qbt[...]).astype(BF)
        prob = prob.astype(BF)
        grad_value = jnp.zeros((2 * PATCH, WIDTH), F32)
        for a in range(3):
            wide = nn(prob, ea[a])
            grad_value = grad_value + jnp.concatenate(
                [d_mixed[a] * wide[:PATCH], d_mixed[a] * wide[PATCH:]], axis=0
            )
        ob[c] = (nt(grad_key, full[PK]) + nt(grad_value.astype(BF), full[PV])).astype(BF)
        return carry

    def own_part(c):
        lanes = pl.ds(pl.multiple_of(h * 128, 128), 128)
        return pltpu.make_async_copy(ob.at[c, :, lanes], rv.at[h, c], own_sem.at[c])

    for c in range(CHUNKS):
        finish(c, 0)
        size = pl.ds(0, 144 if c < CHUNKS - 1 else 80)
        for r, peer in enumerate((sib, over, diag)):
            lanes = pl.ds(pl.multiple_of(peer * 128, 128), 128)
            send(remote(
                ob.at[c, size, lanes], rv.at[h, c, size], a_send.at[c, r], a_recv.at[c, r], (s, peer)
            ))
        own_part(c).start()

    writes = []
    for c in range(CHUNKS):
        size = pl.ds(0, 144 if c < CHUNKS - 1 else 80)
        for r, peer in enumerate((sib, over, diag)):
            place = rv.at[peer, c, size]
            remote(place, place, a_send.at[c, r], a_recv.at[c, r], (s, peer)).wait_recv()
        own_part(c).wait()
        parts = []
        for j in range(4):
            if c < CHUNKS - 1:
                got = rv[j, c].astype(F32)
                parts.append(jnp.concatenate([got[:PATCH], got[PATCH:]], axis=1))
            else:
                parts.append(rv[j, c, 0:80].astype(F32)[:PATCH])
        got = nn(pm[...], jnp.concatenate(parts, axis=0).astype(BF)).astype(BF)
        for i in range(2 if c < CHUNKS - 1 else 1):
            fin[2 * c + i] = got[:, 128 * i:128 * (i + 1)]
        size = pl.ds(2 * c, 2 if c < CHUNKS - 1 else 1)
        copy = pltpu.make_async_copy(fin.at[size], out.at[size], out_sem.at[c])
        copy.start()
        writes.append(copy)
    for copy in writes:
        copy.wait()
    for copy in sent:
        copy.wait_send()


def per_device(levels, latent_query, w_pq, w_pk, w_pv, w_po, gain, wq, wk, wv, wo, cot):
    anywhere = pl.BlockSpec(memory_space=pl.ANY)
    vmem = pl.BlockSpec(memory_space=pltpu.VMEM)
    scratch = [
        pltpu.VMEM((14, 6, 32, WIDTH), BF),
        pltpu.VMEM((3, 6, 32, WIDTH), BF),
        pltpu.VMEM((7, WIDTH, WIDTH), BF),
        pltpu.VMEM((16, WIDTH), F32),
        pltpu.VMEM((4, 16, 128), BF),
        pltpu.VMEM((128, WIDTH), BF),
        pltpu.VMEM((3, 128, WIDTH), BF),
        pltpu.VMEM((3, 128, WIDTH), BF),
        pltpu.VMEM((256, 224), BF),
        pltpu.VMEM((224, 256), BF),
        pltpu.VMEM((288, 288), BF),
        pltpu.VMEM((256, 256), F32),
        pltpu.VMEM((CHUNKS, 144, WIDTH), BF),
        pltpu.VMEM((CHUNKS, 144, WIDTH), BF),
        pltpu.VMEM((CHUNKS, 144, 128), F32),
        pltpu.VMEM((CHUNKS, 144, 128), F32),
        pltpu.VMEM((128, WIDTH), BF),
        pltpu.VMEM((256, WIDTH), BF),
        pltpu.VMEM((128, WIDTH), BF),
        pltpu.VMEM((128, WIDTH), BF),
        pltpu.VMEM((128, WIDTH), BF),
        pltpu.VMEM((128, WIDTH), BF),
    ] + [pltpu.VMEM((256, WIDTH), BF) for _ in range(7)] + [
        pltpu.VMEM((256, WIDTH), F32),
        pltpu.VMEM((256, 128), F32),
        pltpu.VMEM((CHUNKS, 144, WIDTH), BF),
        pltpu.VMEM((4, CHUNKS, 144, 128), BF),
        pltpu.VMEM((14, 288, 128), BF),
    ] + [
        pltpu.SemaphoreType.DMA(shape)
        for shape in (
            (11,), (7, 5), (7, 5), (3,), (3,), (3,), (3,), (CHUNKS, 3), (CHUNKS, 3),
            (CHUNKS,), (CHUNKS,),
        )
    ]
    result = pl.pallas_call(
        kernel,
        out_shape=jax.ShapeDtypeStruct((LEVELS, 288, 128), BF),
        in_specs=[anywhere, vmem, vmem, anywhere, anywhere, anywhere, vmem,
                  anywhere, anywhere, anywhere, anywhere, anywhere],
        out_specs=anywhere,
        scratch_shapes=scratch,
        compiler_params=pltpu.CompilerParams(
            collective_id=0, has_side_effects=True, vmem_limit_bytes=48 * 1024 * 1024
        ),
        name="encoder_backward",
    )(levels, latent_query, w_pq, w_pk, w_pv, w_po, gain.reshape(1, WIDTH), wq, wk, wv, wo, cot)
    return result.reshape(LEVELS, 6, 48, 128)


def solution(mesh):
    placed = (
        P(None, "space", None, None),
        P(),
        P(None, "head"),
        P(None, "head"),
        P(None, "head"),
        P("head", None),
        P(),
        P(None, "head"),
        P(None, "head"),
        P(None, "head"),
        P("head", None),
        P(None, "space", None, None),
    )
    return jax.shard_map(
        per_device,
        mesh=mesh,
        in_specs=placed,
        out_specs=P(None, "space", None, "head"),
        check_vma=False,
    )
```

```python
import functools

import jax
import jax.numpy as jnp
from jax import lax
from jax.experimental import pallas as pl
from jax.experimental.pallas import tpu as pltpu
from jax.sharding import PartitionSpec as P

X_CHIPS = 4
LEVELS = 13
CHUNKS = 4
WIDTH = 512
PART = 40
START = (0, 160, 320, 480)
SIZE = (160, 160, 160, 48)
DEPTH = (4, 4, 4, 1)
SENT = (144, 144, 144, 48)
VMEM_LIMIT = 62 * 1024 * 1024
SCALE = 32 ** (-0.5)
MESH = pl.DeviceIdType.MESH
BF = jnp.bfloat16
F32 = jnp.float32
PK, PV, PO, WO, WQ, WK, WV = range(7)
BY_COLUMN = (True, True, False, False, True, True, True)


def nn(left, right):
    return jnp.dot(left, right, preferred_element_type=F32)


def nt(left, right):
    return lax.dot_general(left, right, (((1,), (1,)), ((), ())), preferred_element_type=F32)


def rows(n):
    return lax.broadcasted_iota(jnp.int32, (n, 1), 0)


def cols(n):
    return lax.broadcasted_iota(jnp.int32, (1, n), 1)


def hot(condition):
    return jnp.where(condition, 1.0, 0.0).astype(BF)


def kernel(
    levels, lq_in, wpq_in, wpk, wpv, wpo, gain_in, wq, wk, wv, wo, cot,
    out,
    lq_ref, wpq_ref, gain_ref, lev, cotx, full, lqs, qbuf, qbt, ea, ead, pack, unpack, pack1, unpack1, bias,
    xs, vs, ps, dps, cot_l, cot_win, lat_l, lat_in, ds_l, ds_in,
    win_q, win_k, win_v, win_o, g_q, g_k, g_v, zs, inv_s, ob, rv, fin,
    loc_sem, w_send, w_recv, q_send, q_recv, e_send, e_recv, a_send, a_recv, own_sem, out_sem,
):
    s = lax.axis_index("space")
    n = lax.axis_size("space")
    h = lax.axis_index("head")
    sib = h + 1 - 2 * lax.rem(h, 2)
    over = lax.rem(h + 2, 4)
    diag = 3 - h
    z_other = s + X_CHIPS - 2 * X_CHIPS * lax.rem(lax.div(s, X_CHIPS), 2)
    prev = lax.rem(s + n - 1, n)
    after = lax.rem(s + 1, n)
    weights = (wpk, wpv, wpo, wo, wq, wk, wv)

    def region(k, head, part):
        if BY_COLUMN[k]:
            along = slice(None) if part is None else pl.ds(256 * part, 256)
            return full.at[k, along, pl.ds(pl.multiple_of(head * 128, 128), 128)]
        if part is None:
            return full.at[k, pl.ds(pl.multiple_of(head * 128, 128), 128)]
        return full.at[k, pl.ds(pl.multiple_of(head * 128 + 64 * part, 64), 64)]

    def shard(k, part):
        if part is None:
            return weights[k]
        size = 256 if BY_COLUMN[k] else 64
        return weights[k].at[pl.ds(size * part, size)]

    def remote(src, dst, send, recv, device):
        return pltpu.make_async_remote_copy(
            src_ref=src, dst_ref=dst, send_sem=send, recv_sem=recv,
            device_id=device, device_id_type=MESH,
        )

    b0 = lax.div(12 * h + 6, 16)
    b1 = lax.rem(b0 + 1, 3)
    base = 12 * h + 6 - 16 * b0
    local = []
    for block, where in ((b0, 0), (b1, 16)):
        at = pl.ds(pl.multiple_of(16 * block, 16), 16)
        local.append((levels.at[:, :, at, :], lev.at[pl.ds(0, LEVELS), :, pl.ds(where, 16), :]))
        local.append((cot.at[:, :, at, :], cotx.at[:, :, pl.ds(where, 16), :]))
    for k in range(7):
        local.append((weights[k], region(k, h, None)))
    for src, dst in ((lq_in, lq_ref), (wpq_in, wpq_ref), (gain_in, gain_ref)):
        local.append((src, dst))
    local = [
        pltpu.make_async_copy(src, dst, loc_sem.at[i]) for i, (src, dst) in enumerate(local)
    ]
    for copy in local:
        copy.start()

    barrier = pltpu.get_barrier_semaphore()
    for device in ((s, sib), (s, over), (s, diag), (z_other, over), (prev, h), (after, h)):
        pl.semaphore_signal(barrier, inc=1, device_id=device, device_id_type=MESH)
    pl.semaphore_wait(barrier, 6)

    sent = []

    def send(copy):
        copy.start()
        sent.append(copy)

    for k in range(7):
        send(remote(shard(k, 0), region(k, h, 0), w_send.at[k, 1], w_recv.at[k, 1], (s, over)))
        send(remote(shard(k, 1), region(k, h, 1), w_send.at[k, 2], w_recv.at[k, 2], (z_other, over)))
        send(remote(shard(k, None), region(k, h, None), w_send.at[k, 0], w_recv.at[k, 0], (s, sib)))

    local[11].wait()
    local[12].wait()
    local[13].wait()
    lqs[...] = jnp.zeros_like(lqs)
    lqs[0:3, :] = lq_ref[...].astype(F32)
    lq16 = lqs[...].astype(BF)
    qbuf[h] = nn(lq16, wpq_ref[...]).astype(BF)
    for r, peer in enumerate((sib, over, diag)):
        send(remote(qbuf.at[h], qbuf.at[h], q_send.at[r], q_recv.at[r], (s, peer)))

    def wait_in(k, i, head, part, peer):
        remote(region(k, head, part), region(k, head, part), w_send.at[k, i], w_recv.at[k, i], (s, peer)).wait_recv()

    def relay(k):
        for part in range(2):
            wait_in(k, 1 + part, over, part, over)
            piece = region(k, over, part)
            send(remote(piece, piece, w_send.at[k, 3 + part], w_recv.at[k, 3 + part], (s, sib)))

    def have(k):
        local[4 + k].wait()
        wait_in(k, 0, sib, None, sib)
        for part in range(2):
            wait_in(k, 3 + part, diag, part, sib)

    lane_head = lax.div(cols(WIDTH), 32)
    for a in range(3):
        ea[a] = hot(rows(128) == a * 16 + lane_head)
        ead[a] = hot(lax.rem(rows(128), 64) == a * 16 + lane_head)
    k_row = lax.div(rows(144), 36) * PART + lax.rem(rows(144), 36)
    pack[...] = hot(k_row == cols(160))
    pack1[...] = hot(jnp.where(rows(48) < 36, rows(48), -1) == cols(PART))
    o_row = lax.rem(rows(288), 144)
    o_lon = lax.rem(lax.rem(o_row, 48) + 42, 48)
    o_cell = lax.div(o_row, 48) * 12 + lax.rem(o_lon, 12)
    unpack[...] = hot(lax.div(o_lon, 12) * 72 + lax.div(rows(288), 144) * 36 + o_cell == cols(288))
    unpack1[...] = hot((lax.div(o_lon, 12) * PART + o_cell)[:144] == cols(160))
    in_half = lax.rem(rows(256), 128)
    pad_key = jnp.logical_or(in_half >= 120, lax.rem(in_half, PART) >= 36)
    crossing = jnp.logical_and((rows(256) < 128) != (cols(256) < 128), s == n - 1)
    bias[...] = jnp.where(jnp.logical_or(pad_key, crossing), -1e30, 0.0).astype(F32)
    lq_row = nn(hot(lax.div(rows(128), PART) == cols(16)), lq16)

    local[0].wait()
    local[2].wait()
    cell = lax.rem(rows(80), PART)
    spot = lax.div(rows(80), PART) * 96 + lax.div(cell, 12) * 32 + base + lax.rem(cell, 12)
    take = hot(jnp.where(cell < 36, spot, -1) == cols(192))
    for c in range(CHUNKS):
        got = [nn(take, lev[4 * c + i].reshape(192, WIDTH)) for i in range(DEPTH[c])]
        for half in range(2):
            part = [one[PART * half:PART * (half + 1)] for one in got]
            if DEPTH[c] == 1:
                part.append(jnp.zeros((8, WIDTH), F32))
            xs[half, START[c]:START[c] + SIZE[c]] = jnp.concatenate(part, axis=0).astype(BF)

    local[1].wait()
    local[3].wait()
    cell = lax.rem(rows(128), PART)
    spot = lax.div(cell, 12) * 32 + base + lax.rem(cell, 12)
    spot = jnp.where(cell < 36, spot, -1000)
    for half in range(2):
        total = None
        for a in range(3):
            here = jnp.where(lax.div(rows(128), PART) == a, spot + half * 96, -1)
            term = nn(hot(here == cols(192)), cotx[a].reshape(192, WIDTH))
            total = term if total is None else total + term
        if half == 0:
            cot_l[...] = total.astype(BF)
            send(remote(cot_l, cot_win.at[pl.ds(128, 128)], e_send.at[0], e_recv.at[0], (prev, h)))
        else:
            cot_win[0:128] = total.astype(BF)

    for r, peer in enumerate((sib, over, diag)):
        remote(qbuf.at[peer], qbuf.at[peer], q_send.at[r], q_recv.at[r], (s, peer)).wait_recv()
    q16 = jnp.concatenate([qbuf[i] for i in range(4)], axis=1)
    q_rows = nn(hot(lax.div(lax.rem(rows(128), 64), 16) == cols(16)), q16)
    qbt[...] = jnp.where(lax.rem(rows(128), 16) == lane_head, q_rows, 0.0).astype(BF)
    relay(PK)
    relay(PV)
    have(PK)
    have(PV)

    def level(ref, half, l):
        return ref[half, PART * l:PART * (l + 1)]

    def spread(value, depth):
        return value[:PART * depth].reshape(depth, PART, value.shape[-1])

    def forward(half):
        for c in range(CHUNKS):
            at = slice(START[c], START[c] + SIZE[c])
            x = xs[half, at]
            key = nn(x, full[PK]).astype(BF)
            ps[half, at] = nt(key, qbt[...]) * SCALE
            vs[half, at] = nn(x, full[PV]).astype(BF)
        top = level(ps, half, 0)
        for l in range(1, LEVELS):
            top = jnp.maximum(top, level(ps, half, l))
        norm = jnp.zeros_like(top)
        for l in range(LEVELS):
            e = jnp.exp(level(ps, half, l) - top)
            ps[half, PART * l:PART * (l + 1)] = e
            norm = norm + e
        inverse = 1.0 / norm
        for l in range(LEVELS):
            ps[half, PART * l:PART * (l + 1)] = level(ps, half, l) * inverse
        ps[half, PART * LEVELS:] = jnp.zeros((8, 128), F32)

    def mix(half):
        total = [jnp.zeros((PART, WIDTH), F32) for _ in range(3)]
        for c in range(CHUNKS):
            at = slice(START[c], START[c] + SIZE[c])
            value = vs[half, at].astype(F32)
            prob = ps[half, at].astype(BF)
            for a in range(3):
                total[a] = total[a] + jnp.sum(spread(nn(prob, ea[a]) * value, DEPTH[c]), axis=0)
        mixed = jnp.concatenate(total + [jnp.zeros((8, WIDTH), F32)], axis=0).astype(BF)
        return (lq_row + nn(mixed, full[PO])).astype(BF)

    forward(0)
    relay(PO)
    have(PO)
    lat_l[...] = mix(0)
    send(remote(lat_l, lat_in, e_send.at[1], e_recv.at[1], (prev, h)))
    relay(WO)
    forward(1)
    relay(WQ)
    latent = mix(1)

    have(WO)
    remote(cot_l, cot_win.at[pl.ds(128, 128)], e_send.at[0], e_recv.at[0], (prev, h)).wait_recv()
    win_o[...] = nt(cot_win[...], full[WO]).astype(BF)
    relay(WK)
    relay(WV)
    remote(lat_l, lat_in, e_send.at[1], e_recv.at[1], (prev, h)).wait_recv()
    z = jnp.concatenate([latent, lat_in[...]], axis=0).astype(F32)
    z = z - jnp.mean(z, axis=-1, keepdims=True)
    inv = lax.rsqrt(jnp.mean(z * z, axis=-1, keepdims=True) + 1e-05)
    z = z * inv
    zs[...] = z
    inv_s[...] = jnp.broadcast_to(inv, (256, 128))
    normed = (z * gain_ref[...]).astype(BF)
    have(WQ)
    win_q[...] = nn(normed, full[WQ]).astype(BF)
    have(WK)
    win_k[...] = nn(normed, full[WK]).astype(BF)
    have(WV)
    win_v[...] = nn(normed, full[WV]).astype(BF)

    def attend(g, carry):
        lanes = pl.ds(pl.multiple_of(g * 128, 128), 128)
        qg, kg, vg, og = win_q[:, lanes], win_k[:, lanes], win_v[:, lanes], win_o[:, lanes]
        kt = kg.astype(F32).T.astype(BF)
        gk = jnp.zeros((256, 128), F32)
        gv = jnp.zeros((256, 128), F32)
        gq = []
        for i in range(4):
            mine = hot(lax.div(cols(128), 32) == i)
            qm = qg * mine
            om = og * mine
            score = nt(kg, qm) * SCALE + bias[...]
            e = jnp.exp(score - jnp.max(score, axis=0, keepdims=True))
            prob = e * (1.0 / jnp.sum(e, axis=0, keepdims=True))
            gv = gv + nn(prob.astype(BF), om)
            dp = nt(vg, om)
            dp = dp - jnp.sum(prob * dp, axis=0, keepdims=True)
            ds = (prob * dp * SCALE).astype(BF)
            gk = gk + nn(ds, qm)
            gq.append(nn(kt[32 * i:32 * i + 32], ds))
        g_k[:, lanes] = gk.astype(BF)
        g_v[:, lanes] = gv.astype(BF)
        g_q[:, lanes] = jnp.concatenate(gq, axis=0).T.astype(BF)
        return carry

    lax.fori_loop(0, 4, attend, 0)

    def shift_grad(at):
        d = nt(g_q[at], full[WQ]) + nt(g_k[at], full[WK]) + nt(g_v[at], full[WV])
        d = d * gain_ref[...]
        z = zs[at]
        return inv_s[at, 0:1] * (
            d - jnp.mean(d, axis=-1, keepdims=True) - z * jnp.mean(d * z, axis=-1, keepdims=True)
        )

    ds_l[...] = shift_grad(slice(128, 256)).astype(BF)
    send(remote(ds_l, ds_in, e_send.at[2], e_recv.at[2], (after, h)))

    low_lanes = cols(128) < 64

    def own_part(half, c):
        lanes = pl.ds(pl.multiple_of(h * 128, 128), 128)
        at = pl.ds(144 * c, SENT[c])
        return pltpu.make_async_copy(ob.at[half, at, lanes], rv.at[h, half, at], own_sem.at[half, c])

    def backward(half, grad):
        d_mixed = nt(grad, full[PO]).astype(BF).astype(F32)
        d_mixed = [d_mixed[PART * a:PART * (a + 1)] for a in range(3)]
        for c in range(CHUNKS):
            size = PART * DEPTH[c]
            value = spread(vs[half, START[c]:START[c] + SIZE[c]].astype(F32), DEPTH[c])
            total = jnp.zeros((size, 128), F32)
            for a in range(3):
                prod = (value * d_mixed[a][None]).reshape(size, WIDTH)
                high = prod.astype(BF)
                low = (prod - high.astype(F32)).astype(BF)
                total = total + nt(high, ead[a]) + nt(low, ead[a])
            dps[START[c]:START[c] + size] = total
        mean = jnp.zeros((PART, 128), F32)
        for l in range(LEVELS):
            mean = mean + level(ps, half, l) * dps[PART * l:PART * (l + 1)]
        for c in range(CHUNKS):
            size = PART * DEPTH[c]
            prob = ps[half, START[c]:START[c] + size]
            dp = spread(dps[START[c]:START[c] + size], DEPTH[c])
            ds = prob * (dp - mean[None]).reshape(size, 128) * SCALE
            high = ds.astype(BF).astype(F32)
            ds = jnp.where(low_lanes, high, ds - high).astype(BF)
            grad_key = nn(ds, qbt[...]).astype(BF)
            prob = prob.astype(BF)
            grad_value = jnp.zeros((DEPTH[c], PART, WIDTH), F32)
            for a in range(3):
                grad_value = grad_value + d_mixed[a][None] * spread(nn(prob, ea[a]), DEPTH[c])
            grad_value = grad_value.reshape(size, WIDTH).astype(BF)
            total = (nt(grad_key, full[PK]) + nt(grad_value, full[PV])).astype(BF)
            total = nn(pack[...] if DEPTH[c] == 4 else pack1[...], total).astype(BF)
            ob[half, 144 * c:144 * c + SENT[c]] = total
            at = pl.ds(144 * c, SENT[c])
            for r, peer in ((1, over), (2, diag), (0, sib)):
                lanes = pl.ds(pl.multiple_of(peer * 128, 128), 128)
                send(remote(
                    ob.at[half, at, lanes], rv.at[h, half, at],
                    a_send.at[half, c, r], a_recv.at[half, c, r], (s, peer),
                ))
            own_part(half, c).start()

    grad = cot_win[0:128].astype(F32) + shift_grad(slice(0, 128))
    backward(1, grad.astype(BF))
    remote(ds_l, ds_in, e_send.at[2], e_recv.at[2], (after, h)).wait_recv()
    grad = cot_l[...].astype(F32) + ds_in[...].astype(F32)
    backward(0, grad.astype(BF))

    writes = []
    for half in (1, 0):
        for c in range(CHUNKS):
            at = pl.ds(144 * c, SENT[c])
            for r, peer in enumerate((sib, over, diag)):
                place = rv.at[peer, half, at]
                remote(place, place, a_send.at[half, c, r], a_recv.at[half, c, r], (s, peer)).wait_recv()
            own_part(half, c).wait()
            parts = []
            for j in range(4):
                got = rv[j, half, 144 * c:144 * c + SENT[c]].astype(F32)
                parts.append(jnp.concatenate([got[:72], got[72:]], axis=1) if DEPTH[c] == 4 else got[:PART])
            got = jnp.concatenate(parts, axis=0).astype(BF)
            got = nn(unpack[...] if DEPTH[c] == 4 else unpack1[...], got).astype(BF)
            for i in range(DEPTH[c]):
                up, along = 144 * (i % 2), 128 * (i // 2)
                fin[4 * c + i, 144 * half:144 * (half + 1)] = got[up:up + 144, along:along + 128]
            at = (pl.ds(4 * c, DEPTH[c]), pl.ds(144 * half, 144))
            copy = pltpu.make_async_copy(fin.at[at], out.at[at], out_sem.at[half, c])
            copy.start()
            writes.append(copy)
    for copy in writes:
        copy.wait()
    for copy in sent:
        copy.wait_send()


def per_device(levels, latent_query, w_pq, w_pk, w_pv, w_po, gain, wq, wk, wv, wo, cot):
    anywhere = pl.BlockSpec(memory_space=pl.ANY)
    scratch = [
        pltpu.VMEM((3, WIDTH), BF),
        pltpu.VMEM((WIDTH, 128), BF),
        pltpu.VMEM((1, WIDTH), F32),
        pltpu.VMEM((LEVELS, 6, 32, WIDTH), BF),
        pltpu.VMEM((3, 6, 32, WIDTH), BF),
        pltpu.VMEM((7, WIDTH, WIDTH), BF),
        pltpu.VMEM((16, WIDTH), F32),
        pltpu.VMEM((4, 16, 128), BF),
        pltpu.VMEM((128, WIDTH), BF),
        pltpu.VMEM((3, 128, WIDTH), BF),
        pltpu.VMEM((3, 128, WIDTH), BF),
        pltpu.VMEM((144, 160), BF),
        pltpu.VMEM((288, 288), BF),
        pltpu.VMEM((48, PART), BF),
        pltpu.VMEM((144, 160), BF),
        pltpu.VMEM((256, 256), F32),
        pltpu.VMEM((2, 528, WIDTH), BF),
        pltpu.VMEM((2, 528, WIDTH), BF),
        pltpu.VMEM((2, 528, 128), F32),
        pltpu.VMEM((528, 128), F32),
        pltpu.VMEM((128, WIDTH), BF),
        pltpu.VMEM((256, WIDTH), BF),
        pltpu.VMEM((128, WIDTH), BF),
        pltpu.VMEM((128, WIDTH), BF),
        pltpu.VMEM((128, WIDTH), BF),
        pltpu.VMEM((128, WIDTH), BF),
    ] + [pltpu.VMEM((256, WIDTH), BF) for _ in range(7)] + [
        pltpu.VMEM((256, WIDTH), F32),
        pltpu.VMEM((256, 128), F32),
        pltpu.VMEM((2, 480, WIDTH), BF),
        pltpu.VMEM((4, 2, 480, 128), BF),
        pltpu.VMEM((LEVELS, 288, 128), BF),
    ] + [
        pltpu.SemaphoreType.DMA(shape)
        for shape in (
            (14,), (7, 5), (7, 5), (3,), (3,), (3,), (3,), (2, CHUNKS, 3), (2, CHUNKS, 3),
            (2, CHUNKS), (2, CHUNKS),
        )
    ]
    result = pl.pallas_call(
        kernel,
        out_shape=jax.ShapeDtypeStruct((LEVELS, 288, 128), BF),
        in_specs=[anywhere] * 12,
        out_specs=anywhere,
        scratch_shapes=scratch,
        compiler_params=pltpu.CompilerParams(
            collective_id=0, has_side_effects=True, vmem_limit_bytes=VMEM_LIMIT
        ),
        name="encoder_backward",
    )(levels, latent_query, w_pq, w_pk, w_pv, w_po, gain.reshape(1, WIDTH), wq, wk, wv, wo, cot)
    return result.reshape(LEVELS, 6, 48, 128)


def solution(mesh):
    placed = (
        P(None, "space", None, None),
        P(),
        P(None, "head"),
        P(None, "head"),
        P(None, "head"),
        P("head", None),
        P(),
        P(None, "head"),
        P(None, "head"),
        P(None, "head"),
        P("head", None),
        P(None, "space", None, None),
    )
    return jax.shard_map(
        per_device,
        mesh=mesh,
        in_specs=placed,
        out_specs=P(None, "space", None, "head"),
        check_vma=False,
    )
```

```python
import functools

import jax
import jax.numpy as jnp
from jax import lax
from jax.experimental import pallas as pl
from jax.experimental.pallas import tpu as pltpu
from jax.sharding import PartitionSpec as P

X_CHIPS = 4
LEVELS = 13
CHUNKS = 4
WIDTH = 512
PART = 40
START = (0, 160, 320, 480)
SIZE = (160, 160, 160, 48)
DEPTH = (4, 4, 4, 1)
SENT = (144, 144, 144, 48)
VMEM_LIMIT = 62 * 1024 * 1024
SCALE = 32 ** (-0.5)
MESH = pl.DeviceIdType.MESH
BF = jnp.bfloat16
F32 = jnp.float32
PK, PV, PO, WO, WQ, WK, WV = range(7)
BY_COLUMN = (True, True, False, False, True, True, True)


def nn(left, right):
    return jnp.dot(left, right, preferred_element_type=F32)


def nt(left, right):
    return lax.dot_general(left, right, (((1,), (1,)), ((), ())), preferred_element_type=F32)


def rows(n):
    return lax.broadcasted_iota(jnp.int32, (n, 1), 0)


def cols(n):
    return lax.broadcasted_iota(jnp.int32, (1, n), 1)


def hot(condition):
    return jnp.where(condition, 1.0, 0.0).astype(BF)


def kernel(
    levels, lq_in, wpq_in, wpk, wpv, wpo, gain_in, wq, wk, wv, wo, cot,
    out,
    lq_ref, wpq_ref, gain_ref, lev, cotx, full, lqs, qbuf, qbt, ea, ead, pack, unpack, pack1, unpack1, bias,
    xs, vs, ps, dps, cot_l, cot_win, lat_l, lat_in, ds_l, ds_in,
    win_q, win_k, win_v, win_o, g_q, g_k, g_v, zs, inv_s, ob, rv, fin,
    loc_sem, w_send, w_recv, q_send, q_recv, e_send, e_recv, a_send, a_recv, own_sem, out_sem,
):
    s = lax.axis_index("space")
    n = lax.axis_size("space")
    h = lax.axis_index("head")
    sib = h + 1 - 2 * lax.rem(h, 2)
    over = lax.rem(h + 2, 4)
    diag = 3 - h
    z_other = s + X_CHIPS - 2 * X_CHIPS * lax.rem(lax.div(s, X_CHIPS), 2)
    prev = lax.rem(s + n - 1, n)
    after = lax.rem(s + 1, n)
    weights = (wpk, wpv, wpo, wo, wq, wk, wv)

    def region(k, head, part=None):
        if BY_COLUMN[k]:
            along = slice(None) if part is None else pl.ds(256 * part, 256)
            return full.at[k, along, pl.ds(pl.multiple_of(head * 128, 128), 128)]
        if part is None:
            return full.at[k, pl.ds(pl.multiple_of(head * 128, 128), 128)]
        return full.at[k, pl.ds(pl.multiple_of(head * 128 + 64 * part, 64), 64)]

    def shard(k, part):
        size = 256 if BY_COLUMN[k] else 64
        return weights[k].at[pl.ds(size * part, size)]

    def remote(src, dst, send, recv, device):
        return pltpu.make_async_remote_copy(
            src_ref=src, dst_ref=dst, send_sem=send, recv_sem=recv,
            device_id=device, device_id_type=MESH,
        )

    b0 = lax.div(12 * h + 6, 16)
    b1 = lax.rem(b0 + 1, 3)
    base = 12 * h + 6 - 16 * b0
    local = []
    for block, where in ((b0, 0), (b1, 16)):
        at = pl.ds(pl.multiple_of(16 * block, 16), 16)
        local.append((levels.at[:, :, at, :], lev.at[pl.ds(0, LEVELS), :, pl.ds(where, 16), :]))
        local.append((cot.at[:, :, at, :], cotx.at[:, :, pl.ds(where, 16), :]))
    for k in range(7):
        local.append((weights[k], region(k, h)))
    for src, dst in ((lq_in, lq_ref), (wpq_in, wpq_ref), (gain_in, gain_ref)):
        local.append((src, dst))
    local = [
        pltpu.make_async_copy(src, dst, loc_sem.at[i]) for i, (src, dst) in enumerate(local)
    ]
    for copy in local:
        copy.start()

    barrier = pltpu.get_barrier_semaphore()
    for device in (
        (s, sib), (s, over), (s, diag), (z_other, over), (prev, h), (after, h),
    ):
        pl.semaphore_signal(barrier, inc=1, device_id=device, device_id_type=MESH)
    pl.semaphore_wait(barrier, 6)

    sent = []

    def send(copy):
        copy.start()
        sent.append(copy)

    for k in range(7):
        send(remote(shard(k, 0), region(k, h, 0), w_send.at[k, 1], w_recv.at[k, 1], (s, over)))
        send(remote(shard(k, 1), region(k, h, 1), w_send.at[k, 2], w_recv.at[k, 2], (z_other, over)))
        send(remote(weights[k], region(k, h), w_send.at[k, 0], w_recv.at[k, 0], (s, sib)))

    local[11].wait()
    local[12].wait()
    local[13].wait()
    lqs[...] = jnp.zeros_like(lqs)
    lqs[0:3, :] = lq_ref[...].astype(F32)
    lq16 = lqs[...].astype(BF)
    qbuf[h] = nn(lq16, wpq_ref[...]).astype(BF)
    for r, peer in enumerate((sib, over, diag)):
        send(remote(qbuf.at[h], qbuf.at[h], q_send.at[r], q_recv.at[r], (s, peer)))

    def wait_in(k, i, piece, device):
        remote(piece, piece, w_send.at[k, i], w_recv.at[k, i], device).wait_recv()

    def relay(k):
        for part, device in enumerate(((s, over), (z_other, over))):
            piece = region(k, over, part)
            wait_in(k, 1 + part, piece, device)
            send(remote(piece, piece, w_send.at[k, 3 + part], w_recv.at[k, 3 + part], (s, sib)))

    def have(k):
        local[4 + k].wait()
        wait_in(k, 0, region(k, sib), (s, sib))
        for part in range(2):
            wait_in(k, 3 + part, region(k, diag, part), (s, sib))

    lane_head = lax.div(cols(WIDTH), 32)
    for a in range(3):
        ea[a] = hot(rows(128) == a * 16 + lane_head)
        ead[a] = hot(lax.rem(rows(128), 64) == a * 16 + lane_head)
    k_row = lax.div(rows(144), 36) * PART + lax.rem(rows(144), 36)
    pack[...] = hot(k_row == cols(160))
    pack1[...] = hot(jnp.where(rows(48) < 36, rows(48), -1) == cols(PART))
    o_row = lax.rem(rows(288), 144)
    o_lon = lax.rem(lax.rem(o_row, 48) + 42, 48)
    o_cell = lax.div(o_row, 48) * 12 + lax.rem(o_lon, 12)
    unpack[...] = hot(lax.div(o_lon, 12) * 72 + lax.div(rows(288), 144) * 36 + o_cell == cols(288))
    unpack1[...] = hot((lax.div(o_lon, 12) * PART + o_cell)[:144] == cols(160))
    in_half = lax.rem(rows(256), 128)
    pad_key = jnp.logical_or(in_half >= 120, lax.rem(in_half, PART) >= 36)
    crossing = jnp.logical_and((rows(256) < 128) != (cols(256) < 128), s == 0)
    bias[...] = jnp.where(jnp.logical_or(pad_key, crossing), -1e30, 0.0).astype(F32)
    lq_row = nn(hot(lax.div(rows(128), PART) == cols(16)), lq16)

    local[0].wait()
    local[2].wait()
    cell = lax.rem(rows(80), PART)
    spot = lax.div(rows(80), PART) * 96 + lax.div(cell, 12) * 32 + base + lax.rem(cell, 12)
    take = hot(jnp.where(cell < 36, spot, -1) == cols(192))
    for c in range(CHUNKS):
        got = [nn(take, lev[4 * c + i].reshape(192, WIDTH)) for i in range(DEPTH[c])]
        for half in range(2):
            part = [one[PART * half:PART * (half + 1)] for one in got]
            if DEPTH[c] == 1:
                part.append(jnp.zeros((8, WIDTH), F32))
            xs[half, START[c]:START[c] + SIZE[c]] = jnp.concatenate(part, axis=0).astype(BF)

    local[1].wait()
    local[3].wait()
    cell = lax.rem(rows(128), PART)
    spot = lax.div(cell, 12) * 32 + base + lax.rem(cell, 12)
    spot = jnp.where(cell < 36, spot, -1000)
    for half in (1, 0):
        total = None
        for a in range(3):
            here = jnp.where(lax.div(rows(128), PART) == a, spot + half * 96, -1)
            term = nn(hot(here == cols(192)), cotx[a].reshape(192, WIDTH))
            total = term if total is None else total + term
        if half == 1:
            cot_l[...] = total.astype(BF)
            send(remote(cot_l, cot_win.at[pl.ds(128, 128)], e_send.at[0], e_recv.at[0], (after, h)))
        else:
            cot_win[0:128] = total.astype(BF)

    for r, peer in enumerate((sib, over, diag)):
        remote(qbuf.at[peer], qbuf.at[peer], q_send.at[r], q_recv.at[r], (s, peer)).wait_recv()
    q16 = jnp.concatenate([qbuf[i] for i in range(4)], axis=1)
    q_rows = nn(hot(lax.div(lax.rem(rows(128), 64), 16) == cols(16)), q16)
    qbt[...] = jnp.where(lax.rem(rows(128), 16) == lane_head, q_rows, 0.0).astype(BF)
    relay(PK)
    relay(PV)
    have(PK)
    have(PV)

    def level(ref, half, l):
        return ref[half, PART * l:PART * (l + 1)]

    def spread(value, depth):
        return value[:PART * depth].reshape(depth, PART, value.shape[-1])

    def forward(half):
        for c in range(CHUNKS):
            at = slice(START[c], START[c] + SIZE[c])
            x = xs[half, at]
            key = nn(x, full[PK]).astype(BF)
            ps[half, at] = nt(key, qbt[...]) * SCALE
            vs[half, at] = nn(x, full[PV]).astype(BF)
        top = level(ps, half, 0)
        for l in range(1, LEVELS):
            top = jnp.maximum(top, level(ps, half, l))
        norm = jnp.zeros_like(top)
        for l in range(LEVELS):
            e = jnp.exp(level(ps, half, l) - top)
            ps[half, PART * l:PART * (l + 1)] = e
            norm = norm + e
        inverse = 1.0 / norm
        for l in range(LEVELS):
            ps[half, PART * l:PART * (l + 1)] = level(ps, half, l) * inverse
        ps[half, PART * LEVELS:] = jnp.zeros((8, 128), F32)

    def mix(half):
        total = [jnp.zeros((PART, WIDTH), F32) for _ in range(3)]
        for c in range(CHUNKS):
            at = slice(START[c], START[c] + SIZE[c])
            value = vs[half, at].astype(F32)
            prob = ps[half, at].astype(BF)
            for a in range(3):
                total[a] = total[a] + jnp.sum(spread(nn(prob, ea[a]) * value, DEPTH[c]), axis=0)
        mixed = jnp.concatenate(total + [jnp.zeros((8, WIDTH), F32)], axis=0).astype(BF)
        return (lq_row + nn(mixed, full[PO])).astype(BF)

    relay(PO)
    forward(1)
    relay(WO)
    relay(WQ)
    have(PO)
    lat_l[...] = mix(1)
    send(remote(lat_l, lat_in, e_send.at[1], e_recv.at[1], (after, h)))
    relay(WK)
    relay(WV)
    forward(0)
    latent = mix(0)

    have(WO)
    remote(cot_l, cot_win.at[pl.ds(128, 128)], e_send.at[0], e_recv.at[0], (after, h)).wait_recv()
    win_o[...] = nt(cot_win[...], full[WO]).astype(BF)
    remote(lat_l, lat_in, e_send.at[1], e_recv.at[1], (after, h)).wait_recv()
    z = jnp.concatenate([latent, lat_in[...]], axis=0).astype(F32)
    z = z - jnp.mean(z, axis=-1, keepdims=True)
    inv = lax.rsqrt(jnp.mean(z * z, axis=-1, keepdims=True) + 1e-05)
    z = z * inv
    zs[...] = z
    inv_s[...] = jnp.broadcast_to(inv, (256, 128))
    normed = (z * gain_ref[...]).astype(BF)
    have(WQ)
    win_q[...] = nn(normed, full[WQ]).astype(BF)
    have(WK)
    win_k[...] = nn(normed, full[WK]).astype(BF)
    have(WV)
    win_v[...] = nn(normed, full[WV]).astype(BF)

    def head_scores(i):
        lanes = slice(128 * (i // 4), 128 * (i // 4) + 128)
        mine = hot(lax.div(cols(128), 32) == i % 4)
        qm, om = win_q[:, lanes] * mine, win_o[:, lanes] * mine
        return qm, om, nt(win_k[:, lanes], qm), nt(win_v[:, lanes], om)

    following = head_scores(0)
    for i in range(16):
        qm, om, score, dp = following
        if i < 15:
            following = head_scores(i + 1)
        if i % 4 == 0:
            lanes = slice(32 * i, 32 * i + 128)
            kt = win_k[:, lanes].astype(F32).T.astype(BF)
            gk = jnp.zeros((256, 128), F32)
            gv = jnp.zeros((256, 128), F32)
            gq = []
        score = score * SCALE + bias[...]
        e = jnp.exp(score - jnp.max(score, axis=0, keepdims=True))
        prob = e * (1.0 / jnp.sum(e, axis=0, keepdims=True))
        dp = dp - jnp.sum(prob * dp, axis=0, keepdims=True)
        ds = (prob * dp * SCALE).astype(BF)
        gv = gv + nn(prob.astype(BF), om)
        gk = gk + nn(ds, qm)
        gq.append(nn(kt[32 * (i % 4):32 * (i % 4) + 32], ds))
        if i % 4 == 3:
            g_k[:, lanes] = gk.astype(BF)
            g_v[:, lanes] = gv.astype(BF)
            g_q[:, lanes] = jnp.concatenate(gq, axis=0).T.astype(BF)

    def shift_grad(at):
        d = nt(g_q[at], full[WQ]) + nt(g_k[at], full[WK]) + nt(g_v[at], full[WV])
        d = d * gain_ref[...]
        z = zs[at]
        return inv_s[at, 0:1] * (
            d - jnp.mean(d, axis=-1, keepdims=True) - z * jnp.mean(d * z, axis=-1, keepdims=True)
        )

    ds_l[...] = shift_grad(slice(128, 256)).astype(BF)
    send(remote(ds_l, ds_in, e_send.at[2], e_recv.at[2], (prev, h)))

    low_lanes = cols(128) < 64

    def own_part(half, c):
        lanes = pl.ds(pl.multiple_of(h * 128, 128), 128)
        at = pl.ds(144 * c, SENT[c])
        return pltpu.make_async_copy(ob.at[half, at, lanes], rv.at[h, half, at], own_sem.at[half, c])

    def backward(half, grad):
        d_mixed = nt(grad, full[PO]).astype(BF).astype(F32)
        d_mixed = [d_mixed[PART * a:PART * (a + 1)] for a in range(3)]
        for c in range(CHUNKS):
            size = PART * DEPTH[c]
            value = spread(vs[half, START[c]:START[c] + SIZE[c]].astype(F32), DEPTH[c])
            total = jnp.zeros((size, 128), F32)
            for a in range(3):
                prod = (value * d_mixed[a][None]).reshape(size, WIDTH)
                high = prod.astype(BF)
                low = (prod - high.astype(F32)).astype(BF)
                total = total + nt(high, ead[a]) + nt(low, ead[a])
            dps[START[c]:START[c] + size] = total
        mean = jnp.zeros((PART, 128), F32)
        for l in range(LEVELS):
            mean = mean + level(ps, half, l) * dps[PART * l:PART * (l + 1)]
        for c in range(CHUNKS):
            size = PART * DEPTH[c]
            prob = ps[half, START[c]:START[c] + size]
            dp = spread(dps[START[c]:START[c] + size], DEPTH[c])
            ds = prob * (dp - mean[None]).reshape(size, 128) * SCALE
            high = ds.astype(BF).astype(F32)
            ds = jnp.where(low_lanes, high, ds - high).astype(BF)
            grad_key = nn(ds, qbt[...]).astype(BF)
            prob = prob.astype(BF)
            grad_value = jnp.zeros((DEPTH[c], PART, WIDTH), F32)
            for a in range(3):
                grad_value = grad_value + d_mixed[a][None] * spread(nn(prob, ea[a]), DEPTH[c])
            grad_value = grad_value.reshape(size, WIDTH).astype(BF)
            total = (nt(grad_key, full[PK]) + nt(grad_value, full[PV])).astype(BF)
            total = nn(pack[...] if DEPTH[c] == 4 else pack1[...], total).astype(BF)
            ob[half, 144 * c:144 * c + SENT[c]] = total
            at = pl.ds(144 * c, SENT[c])
            for r, peer in ((1, over), (2, diag), (0, sib)):
                lanes = pl.ds(pl.multiple_of(peer * 128, 128), 128)
                send(remote(
                    ob.at[half, at, lanes], rv.at[h, half, at],
                    a_send.at[half, c, r], a_recv.at[half, c, r], (s, peer),
                ))
            own_part(half, c).start()

    grad = cot_win[0:128].astype(F32) + shift_grad(slice(0, 128))
    backward(0, grad.astype(BF))
    remote(ds_l, ds_in, e_send.at[2], e_recv.at[2], (prev, h)).wait_recv()
    grad = cot_l[...].astype(F32) + ds_in[...].astype(F32)
    backward(1, grad.astype(BF))

    writes = []
    for half in (0, 1):
        for c in range(CHUNKS):
            at = pl.ds(144 * c, SENT[c])
            for r, peer in enumerate((sib, over, diag)):
                place = rv.at[peer, half, at]
                remote(place, place, a_send.at[half, c, r], a_recv.at[half, c, r], (s, peer)).wait_recv()
            own_part(half, c).wait()
            parts = []
            for j in range(4):
                got = rv[j, half, 144 * c:144 * c + SENT[c]].astype(F32)
                parts.append(jnp.concatenate([got[:72], got[72:]], axis=1) if DEPTH[c] == 4 else got[:PART])
            got = jnp.concatenate(parts, axis=0).astype(BF)
            got = nn(unpack[...] if DEPTH[c] == 4 else unpack1[...], got).astype(BF)
            for i in range(DEPTH[c]):
                up, along = 144 * (i % 2), 128 * (i // 2)
                fin[4 * c + i, 144 * half:144 * (half + 1)] = got[up:up + 144, along:along + 128]
            at = (pl.ds(4 * c, DEPTH[c]), pl.ds(144 * half, 144))
            copy = pltpu.make_async_copy(fin.at[at], out.at[at], out_sem.at[half, c])
            copy.start()
            writes.append(copy)
    for copy in writes:
        copy.wait()
    for copy in sent:
        copy.wait_send()


def per_device(levels, latent_query, w_pq, w_pk, w_pv, w_po, gain, wq, wk, wv, wo, cot):
    anywhere = pl.BlockSpec(memory_space=pl.ANY)
    scratch = [
        pltpu.VMEM((3, WIDTH), BF),
        pltpu.VMEM((WIDTH, 128), BF),
        pltpu.VMEM((1, WIDTH), F32),
        pltpu.VMEM((LEVELS, 6, 32, WIDTH), BF),
        pltpu.VMEM((3, 6, 32, WIDTH), BF),
        pltpu.VMEM((7, WIDTH, WIDTH), BF),
        pltpu.VMEM((16, WIDTH), F32),
        pltpu.VMEM((4, 16, 128), BF),
        pltpu.VMEM((128, WIDTH), BF),
        pltpu.VMEM((3, 128, WIDTH), BF),
        pltpu.VMEM((3, 128, WIDTH), BF),
        pltpu.VMEM((144, 160), BF),
        pltpu.VMEM((288, 288), BF),
        pltpu.VMEM((48, PART), BF),
        pltpu.VMEM((144, 160), BF),
        pltpu.VMEM((256, 256), F32),
        pltpu.VMEM((2, 528, WIDTH), BF),
        pltpu.VMEM((2, 528, WIDTH), BF),
        pltpu.VMEM((2, 528, 128), F32),
        pltpu.VMEM((528, 128), F32),
        pltpu.VMEM((128, WIDTH), BF),
        pltpu.VMEM((256, WIDTH), BF),
        pltpu.VMEM((128, WIDTH), BF),
        pltpu.VMEM((128, WIDTH), BF),
        pltpu.VMEM((128, WIDTH), BF),
        pltpu.VMEM((128, WIDTH), BF),
    ] + [pltpu.VMEM((256, WIDTH), BF) for _ in range(7)] + [
        pltpu.VMEM((256, WIDTH), F32),
        pltpu.VMEM((256, 128), F32),
        pltpu.VMEM((2, 480, WIDTH), BF),
        pltpu.VMEM((4, 2, 480, 128), BF),
        pltpu.VMEM((LEVELS, 288, 128), BF),
    ] + [
        pltpu.SemaphoreType.DMA(shape)
        for shape in (
            (14,), (7, 5), (7, 5), (3,), (3,), (3,), (3,), (2, CHUNKS, 3), (2, CHUNKS, 3),
            (2, CHUNKS), (2, CHUNKS),
        )
    ]
    result = pl.pallas_call(
        kernel,
        out_shape=jax.ShapeDtypeStruct((LEVELS, 288, 128), BF),
        in_specs=[anywhere] * 12,
        out_specs=anywhere,
        scratch_shapes=scratch,
        compiler_params=pltpu.CompilerParams(
            collective_id=0, has_side_effects=True, vmem_limit_bytes=VMEM_LIMIT
        ),
        name="encoder_backward",
    )(levels, latent_query, w_pq, w_pk, w_pv, w_po, gain.reshape(1, WIDTH), wq, wk, wv, wo, cot)
    return result.reshape(LEVELS, 6, 48, 128)


def solution(mesh):
    placed = (
        P(None, "space", None, None),
        P(),
        P(None, "head"),
        P(None, "head"),
        P(None, "head"),
        P("head", None),
        P(),
        P(None, "head"),
        P(None, "head"),
        P(None, "head"),
        P("head", None),
        P(None, "space", None, None),
    )
    return jax.shard_map(
        per_device,
        mesh=mesh,
        in_specs=placed,
        out_specs=P(None, "space", None, "head"),
        check_vma=False,
    )
```

```python
import functools

import jax
import jax.numpy as jnp
from jax import lax
from jax.experimental import pallas as pl
from jax.experimental.pallas import tpu as pltpu
from jax.sharding import PartitionSpec as P

X_CHIPS = 4
LEVELS = 13
CHUNKS = 4
WIDTH = 512
PART = 40
START = (0, 160, 320, 480)
SIZE = (160, 160, 160, 48)
DEPTH = (4, 4, 4, 1)
SENT = (144, 144, 144, 48)
VMEM_LIMIT = 60 * 1024 * 1024
SCALE = 32 ** (-0.5)
MESH = pl.DeviceIdType.MESH
BF = jnp.bfloat16
F32 = jnp.float32
PK, PV, PO, WO, WQ, WK, WV = range(7)
BY_COLUMN = (True, True, False, False, True, True, True)


def nn(left, right):
    return jnp.dot(left, right, preferred_element_type=F32)


def nt(left, right):
    return lax.dot_general(left, right, (((1,), (1,)), ((), ())), preferred_element_type=F32)


def rows(n):
    return lax.broadcasted_iota(jnp.int32, (n, 1), 0)


def cols(n):
    return lax.broadcasted_iota(jnp.int32, (1, n), 1)


def hot(condition):
    return jnp.where(condition, 1.0, 0.0).astype(BF)


def kernel(
    levels, lq_in, wpq_in, wpk, wpv, wpo, gain_in, wq, wk, wv, wo, cot,
    out,
    lq_ref, wpq_ref, gain_ref, lev, cotx, full, lqs, qbuf, qbt, ea, ead, pack, unpack, pack1, unpack1, bias,
    xs, vs, ps, dps, cot_l, cot_win, lat_l, lat_in, ds_l, ds_in,
    win_q, win_k, win_v, win_o, g_q, g_k, g_v, zs, inv_s, ob, rv,
    loc_sem, w_send, w_recv, q_send, q_recv, e_send, e_recv, a_send, a_recv, own_sem,
):
    s = lax.axis_index("space")
    n = lax.axis_size("space")
    h = lax.axis_index("head")
    sib = h + 1 - 2 * lax.rem(h, 2)
    over = lax.rem(h + 2, 4)
    diag = 3 - h
    z_other = s + X_CHIPS - 2 * X_CHIPS * lax.rem(lax.div(s, X_CHIPS), 2)
    prev = lax.rem(s + n - 1, n)
    after = lax.rem(s + 1, n)
    weights = (wpk, wpv, wpo, wo, wq, wk, wv)

    def region(k, head, part=None):
        if BY_COLUMN[k]:
            along = slice(None) if part is None else pl.ds(256 * part, 256)
            return full.at[k, along, pl.ds(pl.multiple_of(head * 128, 128), 128)]
        if part is None:
            return full.at[k, pl.ds(pl.multiple_of(head * 128, 128), 128)]
        return full.at[k, pl.ds(pl.multiple_of(head * 128 + 64 * part, 64), 64)]

    def shard(k, part):
        size = 256 if BY_COLUMN[k] else 64
        return weights[k].at[pl.ds(size * part, size)]

    def remote(src, dst, send, recv, device):
        return pltpu.make_async_remote_copy(
            src_ref=src, dst_ref=dst, send_sem=send, recv_sem=recv,
            device_id=device, device_id_type=MESH,
        )

    b0 = lax.div(12 * h + 6, 16)
    b1 = lax.rem(b0 + 1, 3)
    base = 12 * h + 6 - 16 * b0
    local = []
    for block, where in ((b0, 0), (b1, 16)):
        at = pl.ds(pl.multiple_of(16 * block, 16), 16)
        local.append((levels.at[:, :, at, :], lev.at[pl.ds(0, LEVELS), :, pl.ds(where, 16), :]))
        local.append((cot.at[:, :, at, :], cotx.at[:, :, pl.ds(where, 16), :]))
    for k in range(7):
        local.append((weights[k], region(k, h)))
    for src, dst in ((lq_in, lq_ref), (wpq_in, wpq_ref), (gain_in, gain_ref)):
        local.append((src, dst))
    local = [
        pltpu.make_async_copy(src, dst, loc_sem.at[i]) for i, (src, dst) in enumerate(local)
    ]
    for copy in local:
        copy.start()

    barrier = pltpu.get_barrier_semaphore()
    for device in (
        (s, sib), (s, over), (s, diag), (z_other, over), (prev, h), (after, h),
    ):
        pl.semaphore_signal(barrier, inc=1, device_id=device, device_id_type=MESH)
    pl.semaphore_wait(barrier, 6)

    sent = []

    def send(copy):
        copy.start()
        sent.append(copy)

    def scatter(k):
        send(remote(shard(k, 0), region(k, h, 0), w_send.at[k, 1], w_recv.at[k, 1], (s, over)))
        send(remote(shard(k, 1), region(k, h, 1), w_send.at[k, 2], w_recv.at[k, 2], (z_other, over)))
        send(remote(weights[k], region(k, h), w_send.at[k, 0], w_recv.at[k, 0], (s, sib)))

    for k in (PK, PV):
        scatter(k)

    local[11].wait()
    local[12].wait()
    local[13].wait()
    lqs[...] = jnp.zeros_like(lqs)
    lqs[0:3, :] = lq_ref[...].astype(F32)
    lq16 = lqs[...].astype(BF)
    qbuf[h] = nn(lq16, wpq_ref[...]).astype(BF)
    for r, peer in enumerate((sib, over, diag)):
        send(remote(qbuf.at[h], qbuf.at[h], q_send.at[r], q_recv.at[r], (s, peer)))
    for k in (PO, WO, WQ, WK, WV):
        scatter(k)

    def wait_in(k, i, piece, device):
        remote(piece, piece, w_send.at[k, i], w_recv.at[k, i], device).wait_recv()

    def relay(k):
        for part, device in enumerate(((s, over), (z_other, over))):
            piece = region(k, over, part)
            wait_in(k, 1 + part, piece, device)
            send(remote(piece, piece, w_send.at[k, 3 + part], w_recv.at[k, 3 + part], (s, sib)))

    def have(k):
        local[4 + k].wait()
        wait_in(k, 0, region(k, sib), (s, sib))
        for part in range(2):
            wait_in(k, 3 + part, region(k, diag, part), (s, sib))

    lane_head = lax.div(cols(WIDTH), 32)
    for a in range(3):
        ea[a] = hot(rows(128) == a * 16 + lane_head)
        ead[a] = hot(lax.rem(rows(128), 64) == a * 16 + lane_head)
    k_row = lax.div(rows(144), 36) * PART + lax.rem(rows(144), 36)
    pack[...] = hot(k_row == cols(160))
    pack1[...] = hot(jnp.where(rows(48) < 36, rows(48), -1) == cols(PART))
    o_row = lax.rem(rows(288), 144)
    o_lon = lax.rem(lax.rem(o_row, 48) + 42, 48)
    o_cell = lax.div(o_row, 48) * 12 + lax.rem(o_lon, 12)
    unpack[...] = hot(lax.div(o_lon, 12) * 72 + lax.div(rows(288), 144) * 36 + o_cell == cols(288))
    unpack1[...] = hot((lax.div(o_lon, 12) * PART + o_cell)[:144] == cols(160))
    in_half = lax.rem(rows(256), 128)
    pad_key = jnp.logical_or(in_half >= 120, lax.rem(in_half, PART) >= 36)
    crossing = jnp.logical_and((rows(256) < 128) != (cols(256) < 128), s == 0)
    bias[...] = jnp.where(jnp.logical_or(pad_key, crossing), -1e30, 0.0).astype(F32)
    lq_row = nn(hot(lax.div(rows(128), PART) == cols(16)), lq16)

    local[0].wait()
    local[2].wait()
    cell = lax.rem(rows(80), PART)
    spot = lax.div(rows(80), PART) * 96 + lax.div(cell, 12) * 32 + base + lax.rem(cell, 12)
    take = hot(jnp.where(cell < 36, spot, -1) == cols(192))
    for c in range(CHUNKS):
        got = [nn(take, lev[4 * c + i].reshape(192, WIDTH)) for i in range(DEPTH[c])]
        for half in range(2):
            part = [one[PART * half:PART * (half + 1)] for one in got]
            if DEPTH[c] == 1:
                part.append(jnp.zeros((8, WIDTH), F32))
            xs[half, START[c]:START[c] + SIZE[c]] = jnp.concatenate(part, axis=0).astype(BF)

    local[1].wait()
    local[3].wait()
    cell = lax.rem(rows(128), PART)
    spot = lax.div(cell, 12) * 32 + base + lax.rem(cell, 12)
    spot = jnp.where(cell < 36, spot, -1000)
    for half in (1, 0):
        total = None
        for a in range(3):
            here = jnp.where(lax.div(rows(128), PART) == a, spot + half * 96, -1)
            term = nn(hot(here == cols(192)), cotx[a].reshape(192, WIDTH))
            total = term if total is None else total + term
        if half == 1:
            cot_l[...] = total.astype(BF)
            send(remote(cot_l, cot_win.at[pl.ds(128, 128)], e_send.at[0], e_recv.at[0], (after, h)))
        else:
            cot_win[0:128] = total.astype(BF)

    for r, peer in enumerate((sib, over, diag)):
        remote(qbuf.at[peer], qbuf.at[peer], q_send.at[r], q_recv.at[r], (s, peer)).wait_recv()
    q16 = jnp.concatenate([qbuf[i] for i in range(4)], axis=1)
    q_rows = nn(hot(lax.div(lax.rem(rows(128), 64), 16) == cols(16)), q16)
    qbt[...] = jnp.where(lax.rem(rows(128), 16) == lane_head, q_rows, 0.0).astype(BF)
    relay(PK)
    relay(PV)
    have(PK)
    have(PV)

    def level(ref, half, l):
        return ref[half, PART * l:PART * (l + 1)]

    def spread(value, depth):
        return value[:PART * depth].reshape(depth, PART, value.shape[-1])

    def forward(half):
        for c in range(CHUNKS):
            at = slice(START[c], START[c] + SIZE[c])
            x = xs[half, at]
            key = nn(x, full[PK]).astype(BF)
            ps[half, at] = nt(key, qbt[...]) * SCALE
            vs[half, at] = nn(x, full[PV]).astype(BF)
        top = level(ps, half, 0)
        for l in range(1, LEVELS):
            top = jnp.maximum(top, level(ps, half, l))
        norm = jnp.zeros_like(top)
        for l in range(LEVELS):
            e = jnp.exp(level(ps, half, l) - top)
            ps[half, PART * l:PART * (l + 1)] = e
            norm = norm + e
        inverse = 1.0 / norm
        for l in range(LEVELS):
            ps[half, PART * l:PART * (l + 1)] = level(ps, half, l) * inverse
        ps[half, PART * LEVELS:] = jnp.zeros((8, 128), F32)

    def mix(half):
        total = [jnp.zeros((PART, WIDTH), F32) for _ in range(3)]
        for c in range(CHUNKS):
            at = slice(START[c], START[c] + SIZE[c])
            value = vs[half, at].astype(F32)
            prob = ps[half, at].astype(BF)
            for a in range(3):
                total[a] = total[a] + jnp.sum(spread(nn(prob, ea[a]) * value, DEPTH[c]), axis=0)
        mixed = jnp.concatenate(total + [jnp.zeros((8, WIDTH), F32)], axis=0).astype(BF)
        return (lq_row + nn(mixed, full[PO])).astype(BF)

    relay(PO)
    forward(1)
    relay(WO)
    relay(WQ)
    have(PO)
    lat_l[...] = mix(1)
    send(remote(lat_l, lat_in, e_send.at[1], e_recv.at[1], (after, h)))
    relay(WK)
    relay(WV)
    forward(0)
    latent = mix(0)

    have(WO)
    remote(cot_l, cot_win.at[pl.ds(128, 128)], e_send.at[0], e_recv.at[0], (after, h)).wait_recv()
    win_o[...] = nt(cot_win[...], full[WO]).astype(BF)
    remote(lat_l, lat_in, e_send.at[1], e_recv.at[1], (after, h)).wait_recv()
    z = jnp.concatenate([latent, lat_in[...]], axis=0).astype(F32)
    z = z - jnp.mean(z, axis=-1, keepdims=True)
    inv = lax.rsqrt(jnp.mean(z * z, axis=-1, keepdims=True) + 1e-05)
    z = z * inv
    zs[...] = z
    inv_s[...] = jnp.broadcast_to(inv, (256, 128))
    normed = (z * gain_ref[...]).astype(BF)
    have(WQ)
    win_q[...] = nn(normed, full[WQ]).astype(BF)
    have(WK)
    win_k[...] = nn(normed, full[WK]).astype(BF)
    have(WV)
    win_v[...] = nn(normed, full[WV]).astype(BF)

    def head_scores(i):
        lanes = slice(128 * (i // 4), 128 * (i // 4) + 128)
        mine = hot(lax.div(cols(128), 32) == i % 4)
        qm, om = win_q[:, lanes] * mine, win_o[:, lanes] * mine
        return qm, om, nt(win_k[:, lanes], qm), nt(win_v[:, lanes], om)

    following = head_scores(0)
    for i in range(16):
        qm, om, score, dp = following
        if i < 15:
            following = head_scores(i + 1)
        if i % 4 == 0:
            lanes = slice(32 * i, 32 * i + 128)
            kt = win_k[:, lanes].astype(F32).T.astype(BF)
            gk = jnp.zeros((256, 128), F32)
            gv = jnp.zeros((256, 128), F32)
            gq = []
        score = score * SCALE + bias[...]
        e = jnp.exp(score - jnp.max(score, axis=0, keepdims=True))
        prob = e * (1.0 / jnp.sum(e, axis=0, keepdims=True))
        dp = dp - jnp.sum(prob * dp, axis=0, keepdims=True)
        ds = (prob * dp * SCALE).astype(BF)
        gv = gv + nn(prob.astype(BF), om)
        gk = gk + nn(ds, qm)
        gq.append(nn(kt[32 * (i % 4):32 * (i % 4) + 32], ds))
        if i % 4 == 3:
            g_k[:, lanes] = gk.astype(BF)
            g_v[:, lanes] = gv.astype(BF)
            g_q[:, lanes] = jnp.concatenate(gq, axis=0).T.astype(BF)

    def shift_grad(at):
        d = nt(g_q[at], full[WQ]) + nt(g_k[at], full[WK]) + nt(g_v[at], full[WV])
        d = d * gain_ref[...]
        z = zs[at]
        return inv_s[at, 0:1] * (
            d - jnp.mean(d, axis=-1, keepdims=True) - z * jnp.mean(d * z, axis=-1, keepdims=True)
        )

    ds_l[...] = shift_grad(slice(128, 256)).astype(BF)
    send(remote(ds_l, ds_in, e_send.at[2], e_recv.at[2], (prev, h)))

    low_lanes = cols(128) < 64

    def own_part(half, c):
        lanes = pl.ds(pl.multiple_of(h * 128, 128), 128)
        at = pl.ds(144 * c, SENT[c])
        return pltpu.make_async_copy(ob.at[half, at, lanes], rv.at[h, half, at], own_sem.at[half, c])

    def backward(half, grad):
        d_mixed = nt(grad, full[PO]).astype(BF).astype(F32)
        d_mixed = [d_mixed[PART * a:PART * (a + 1)] for a in range(3)]
        for c in range(CHUNKS):
            size = PART * DEPTH[c]
            value = spread(vs[half, START[c]:START[c] + SIZE[c]].astype(F32), DEPTH[c])
            total = jnp.zeros((size, 128), F32)
            for a in range(3):
                prod = (value * d_mixed[a][None]).reshape(size, WIDTH)
                high = prod.astype(BF)
                low = (prod - high.astype(F32)).astype(BF)
                total = total + nt(high, ead[a]) + nt(low, ead[a])
            dps[START[c]:START[c] + size] = total
        mean = jnp.zeros((PART, 128), F32)
        for l in range(LEVELS):
            mean = mean + level(ps, half, l) * dps[PART * l:PART * (l + 1)]
        for c in range(CHUNKS):
            size = PART * DEPTH[c]
            prob = ps[half, START[c]:START[c] + size]
            dp = spread(dps[START[c]:START[c] + size], DEPTH[c])
            ds = prob * (dp - mean[None]).reshape(size, 128) * SCALE
            high = ds.astype(BF).astype(F32)
            ds = jnp.where(low_lanes, high, ds - high).astype(BF)
            grad_key = nn(ds, qbt[...]).astype(BF)
            prob = prob.astype(BF)
            grad_value = jnp.zeros((DEPTH[c], PART, WIDTH), F32)
            for a in range(3):
                grad_value = grad_value + d_mixed[a][None] * spread(nn(prob, ea[a]), DEPTH[c])
            grad_value = grad_value.reshape(size, WIDTH).astype(BF)
            total = (nt(grad_key, full[PK]) + nt(grad_value, full[PV])).astype(BF)
            total = nn(pack[...] if DEPTH[c] == 4 else pack1[...], total).astype(BF)
            ob[half, 144 * c:144 * c + SENT[c]] = total
            at = pl.ds(144 * c, SENT[c])
            for r, peer in ((1, over), (2, diag), (0, sib)):
                lanes = pl.ds(pl.multiple_of(peer * 128, 128), 128)
                send(remote(
                    ob.at[half, at, lanes], rv.at[h, half, at],
                    a_send.at[half, c, r], a_recv.at[half, c, r], (s, peer),
                ))
            own_part(half, c).start()

    grad = cot_win[0:128].astype(F32) + shift_grad(slice(0, 128))
    backward(0, grad.astype(BF))
    remote(ds_l, ds_in, e_send.at[2], e_recv.at[2], (prev, h)).wait_recv()
    grad = cot_l[...].astype(F32) + ds_in[...].astype(F32)
    backward(1, grad.astype(BF))

    for half in (0, 1):
        for c in range(CHUNKS):
            at = pl.ds(144 * c, SENT[c])
            for r, peer in enumerate((sib, over, diag)):
                place = rv.at[peer, half, at]
                remote(place, place, a_send.at[half, c, r], a_recv.at[half, c, r], (s, peer)).wait_recv()
            own_part(half, c).wait()
            parts = []
            for j in range(4):
                got = rv[j, half, 144 * c:144 * c + SENT[c]].astype(F32)
                parts.append(jnp.concatenate([got[:72], got[72:]], axis=1) if DEPTH[c] == 4 else got[:PART])
            got = jnp.concatenate(parts, axis=0).astype(BF)
            got = nn(unpack[...] if DEPTH[c] == 4 else unpack1[...], got).astype(BF)
            for i in range(DEPTH[c]):
                up, along = 144 * (i % 2), 128 * (i // 2)
                out[4 * c + i, 144 * half:144 * (half + 1)] = got[up:up + 144, along:along + 128]
    for copy in sent:
        copy.wait_send()


def per_device(levels, latent_query, w_pq, w_pk, w_pv, w_po, gain, wq, wk, wv, wo, cot):
    anywhere = pl.BlockSpec(memory_space=pl.ANY)
    scratch = [
        pltpu.VMEM((3, WIDTH), BF),
        pltpu.VMEM((WIDTH, 128), BF),
        pltpu.VMEM((1, WIDTH), F32),
        pltpu.VMEM((LEVELS, 6, 32, WIDTH), BF),
        pltpu.VMEM((3, 6, 32, WIDTH), BF),
        pltpu.VMEM((7, WIDTH, WIDTH), BF),
        pltpu.VMEM((16, WIDTH), F32),
        pltpu.VMEM((4, 16, 128), BF),
        pltpu.VMEM((128, WIDTH), BF),
        pltpu.VMEM((3, 128, WIDTH), BF),
        pltpu.VMEM((3, 128, WIDTH), BF),
        pltpu.VMEM((144, 160), BF),
        pltpu.VMEM((288, 288), BF),
        pltpu.VMEM((48, PART), BF),
        pltpu.VMEM((144, 160), BF),
        pltpu.VMEM((256, 256), F32),
        pltpu.VMEM((2, 528, WIDTH), BF),
        pltpu.VMEM((2, 528, WIDTH), BF),
        pltpu.VMEM((2, 528, 128), F32),
        pltpu.VMEM((528, 128), F32),
        pltpu.VMEM((128, WIDTH), BF),
        pltpu.VMEM((256, WIDTH), BF),
        pltpu.VMEM((128, WIDTH), BF),
        pltpu.VMEM((128, WIDTH), BF),
        pltpu.VMEM((128, WIDTH), BF),
        pltpu.VMEM((128, WIDTH), BF),
    ] + [pltpu.VMEM((256, WIDTH), BF) for _ in range(7)] + [
        pltpu.VMEM((256, WIDTH), F32),
        pltpu.VMEM((256, 128), F32),
        pltpu.VMEM((2, 480, WIDTH), BF),
        pltpu.VMEM((4, 2, 480, 128), BF),
    ] + [
        pltpu.SemaphoreType.DMA(shape)
        for shape in (
            (14,), (7, 5), (7, 5), (3,), (3,), (3,), (3,), (2, CHUNKS, 3), (2, CHUNKS, 3),
            (2, CHUNKS),
        )
    ]
    result = pl.pallas_call(
        kernel,
        out_shape=pltpu.VMEM((LEVELS, 288, 128), BF),
        in_specs=[anywhere] * 12,
        out_specs=pl.BlockSpec(memory_space=pltpu.VMEM),
        scratch_shapes=scratch,
        compiler_params=pltpu.CompilerParams(
            collective_id=0, has_side_effects=True, vmem_limit_bytes=VMEM_LIMIT
        ),
        name="encoder_backward",
    )(levels, latent_query, w_pq, w_pk, w_pv, w_po, gain.reshape(1, WIDTH), wq, wk, wv, wo, cot)
    return result.reshape(LEVELS, 6, 48, 128)


def solution(mesh):
    placed = (
        P(None, "space", None, None),
        P(),
        P(None, "head"),
        P(None, "head"),
        P(None, "head"),
        P("head", None),
        P(),
        P(None, "head"),
        P(None, "head"),
        P(None, "head"),
        P("head", None),
        P(None, "space", None, None),
    )
    return jax.shard_map(
        per_device,
        mesh=mesh,
        in_specs=placed,
        out_specs=P(None, "space", None, "head"),
        check_vma=False,
    )
```

```python
import functools

import jax
import jax.numpy as jnp
from jax import lax
from jax.experimental import pallas as pl
from jax.experimental.pallas import tpu as pltpu
from jax.sharding import PartitionSpec as P

X_CHIPS = 4
LEVELS = 13
CHUNKS = 4
WIDTH = 512
PART = 40
START = (0, 160, 320, 480)
SIZE = (160, 160, 160, 48)
DEPTH = (4, 4, 4, 1)
SENT = (144, 144, 144, 48)
VMEM_LIMIT = 60 * 1024 * 1024
SCALE = 32 ** (-0.5)
LOG2E = 1.4426950408889634
MESH = pl.DeviceIdType.MESH
BF = jnp.bfloat16
F32 = jnp.float32
PK, PV, PO, WO, WQ, WK, WV = range(7)
BY_COLUMN = (True, True, False, False, True, True, True)


def nn(left, right):
    return jnp.dot(left, right, preferred_element_type=F32)


def nt(left, right):
    return lax.dot_general(left, right, (((1,), (1,)), ((), ())), preferred_element_type=F32)


def rows(n):
    return lax.broadcasted_iota(jnp.int32, (n, 1), 0)


def cols(n):
    return lax.broadcasted_iota(jnp.int32, (1, n), 1)


def hot(condition):
    return jnp.where(condition, 1.0, 0.0).astype(BF)


def kernel(
    levels, lq_in, wpq_in, wpk, wpv, wpo, gain_in, wq, wk, wv, wo, cot,
    out,
    lq_ref, wpq_ref, gain_ref, lev, cotx, full, lqs, qbuf, qbt, ea, ead, pack, unpack, pack1, unpack1, bias,
    xs, vs, ps, dps, cot_l, cot_win, lat_l, lat_in, ds_l, ds_in,
    win_q, win_k, win_v, win_o, g_q, g_k, g_v, zs, inv_s, ob, rv,
    loc_sem, w_send, w_recv, q_send, q_recv, e_send, e_recv, a_send, a_recv, own_sem,
):
    s = lax.axis_index("space")
    n = lax.axis_size("space")
    h = lax.axis_index("head")
    sib = h + 1 - 2 * lax.rem(h, 2)
    over = lax.rem(h + 2, 4)
    diag = 3 - h
    z_other = s + X_CHIPS - 2 * X_CHIPS * lax.rem(lax.div(s, X_CHIPS), 2)
    prev = lax.rem(s + n - 1, n)
    after = lax.rem(s + 1, n)
    weights = (wpk, wpv, wpo, wo, wq, wk, wv)

    def region(k, head, part=None):
        if BY_COLUMN[k]:
            along = slice(None) if part is None else pl.ds(256 * part, 256)
            return full.at[k, along, pl.ds(pl.multiple_of(head * 128, 128), 128)]
        if part is None:
            return full.at[k, pl.ds(pl.multiple_of(head * 128, 128), 128)]
        return full.at[k, pl.ds(pl.multiple_of(head * 128 + 64 * part, 64), 64)]

    def shard(k, part):
        size = 256 if BY_COLUMN[k] else 64
        return weights[k].at[pl.ds(size * part, size)]

    def remote(src, dst, send, recv, device):
        return pltpu.make_async_remote_copy(
            src_ref=src, dst_ref=dst, send_sem=send, recv_sem=recv,
            device_id=device, device_id_type=MESH,
        )

    barrier = pltpu.get_barrier_semaphore()
    for device in (
        (s, sib), (s, over), (s, diag), (z_other, over), (prev, h), (after, h),
    ):
        pl.semaphore_signal(barrier, inc=1, device_id=device, device_id_type=MESH)

    b0 = lax.div(12 * h + 6, 16)
    b1 = lax.rem(b0 + 1, 3)
    base = 12 * h + 6 - 16 * b0
    local = []
    for block, where in ((b0, 0), (b1, 16)):
        at = pl.ds(pl.multiple_of(16 * block, 16), 16)
        local.append((levels.at[:, :, at, :], lev.at[pl.ds(0, LEVELS), :, pl.ds(where, 16), :]))
        local.append((cot.at[:, :, at, :], cotx.at[:, :, pl.ds(where, 16), :]))
    for k in range(7):
        local.append((weights[k], region(k, h)))
    for src, dst in ((lq_in, lq_ref), (wpq_in, wpq_ref), (gain_in, gain_ref)):
        local.append((src, dst))
    local = [
        pltpu.make_async_copy(src, dst, loc_sem.at[i]) for i, (src, dst) in enumerate(local)
    ]
    for copy in local[11:] + local[:11]:
        copy.start()

    local[11].wait()
    local[12].wait()
    local[13].wait()
    lqs[...] = jnp.zeros_like(lqs)
    lqs[0:3, :] = lq_ref[...].astype(F32)
    lq16 = lqs[...].astype(BF)
    qbuf[h] = nn(lq16, wpq_ref[...]).astype(BF)

    pl.semaphore_wait(barrier, 6)

    sent = []

    def send(copy):
        copy.start()
        sent.append(copy)

    def scatter(k):
        send(remote(shard(k, 0), region(k, h, 0), w_send.at[k, 1], w_recv.at[k, 1], (s, over)))
        send(remote(shard(k, 1), region(k, h, 1), w_send.at[k, 2], w_recv.at[k, 2], (z_other, over)))
        send(remote(weights[k], region(k, h), w_send.at[k, 0], w_recv.at[k, 0], (s, sib)))

    for r, peer in enumerate((sib, over, diag)):
        send(remote(qbuf.at[h], qbuf.at[h], q_send.at[r], q_recv.at[r], (s, peer)))
    for k in range(7):
        scatter(k)

    def wait_in(k, i, piece, device):
        remote(piece, piece, w_send.at[k, i], w_recv.at[k, i], device).wait_recv()

    def relay(k):
        for part, device in enumerate(((s, over), (z_other, over))):
            piece = region(k, over, part)
            wait_in(k, 1 + part, piece, device)
            send(remote(piece, piece, w_send.at[k, 3 + part], w_recv.at[k, 3 + part], (s, sib)))

    def have(k):
        local[4 + k].wait()
        wait_in(k, 0, region(k, sib), (s, sib))
        for part in range(2):
            wait_in(k, 3 + part, region(k, diag, part), (s, sib))

    lane_head = lax.div(cols(WIDTH), 32)
    for a in range(3):
        ea[a] = hot(rows(128) == a * 16 + lane_head)
        ead[a] = hot(lax.rem(rows(128), 64) == a * 16 + lane_head)
    k_row = lax.div(rows(144), 36) * PART + lax.rem(rows(144), 36)
    pack[...] = hot(k_row == cols(160))
    pack1[...] = hot(jnp.where(rows(48) < 36, rows(48), -1) == cols(PART))
    o_row = lax.rem(rows(288), 144)
    o_lon = lax.rem(lax.rem(o_row, 48) + 42, 48)
    o_cell = lax.div(o_row, 48) * 12 + lax.rem(o_lon, 12)
    unpack[...] = hot(lax.div(o_lon, 12) * 72 + lax.div(rows(288), 144) * 36 + o_cell == cols(288))
    unpack1[...] = hot((lax.div(o_lon, 12) * PART + o_cell)[:144] == cols(160))
    in_half = lax.rem(rows(256), 128)
    pad_key = jnp.logical_or(in_half >= 120, lax.rem(in_half, PART) >= 36)
    crossing = jnp.logical_and((rows(256) < 128) != (cols(256) < 128), s == 0)
    bias[...] = jnp.where(jnp.logical_or(pad_key, crossing), -1e30, 0.0).astype(F32)
    lq_row = nn(hot(lax.div(rows(128), PART) == cols(16)), lq16)

    local[0].wait()
    local[2].wait()
    cell = lax.rem(rows(80), PART)
    spot = lax.div(rows(80), PART) * 96 + lax.div(cell, 12) * 32 + base + lax.rem(cell, 12)
    take = hot(jnp.where(cell < 36, spot, -1) == cols(192))
    for c in range(CHUNKS):
        got = [nn(take, lev[4 * c + i].reshape(192, WIDTH)) for i in range(DEPTH[c])]
        for half in range(2):
            part = [one[PART * half:PART * (half + 1)] for one in got]
            if DEPTH[c] == 1:
                part.append(jnp.zeros((8, WIDTH), F32))
            xs[half, START[c]:START[c] + SIZE[c]] = jnp.concatenate(part, axis=0).astype(BF)

    local[1].wait()
    local[3].wait()
    cell = lax.rem(rows(128), PART)
    spot = lax.div(cell, 12) * 32 + base + lax.rem(cell, 12)
    spot = jnp.where(cell < 36, spot, -1000)
    for half in (1, 0):
        total = None
        for a in range(3):
            here = jnp.where(lax.div(rows(128), PART) == a, spot + half * 96, -1)
            term = nn(hot(here == cols(192)), cotx[a].reshape(192, WIDTH))
            total = term if total is None else total + term
        if half == 1:
            cot_l[...] = total.astype(BF)
            send(remote(cot_l, cot_win.at[pl.ds(128, 128)], e_send.at[0], e_recv.at[0], (after, h)))
        else:
            cot_win[0:128] = total.astype(BF)

    for r, peer in enumerate((sib, over, diag)):
        remote(qbuf.at[peer], qbuf.at[peer], q_send.at[r], q_recv.at[r], (s, peer)).wait_recv()
    q16 = jnp.concatenate([qbuf[i] for i in range(4)], axis=1)
    q_rows = nn(hot(lax.div(lax.rem(rows(128), 64), 16) == cols(16)), q16)
    qbt[...] = jnp.where(lax.rem(rows(128), 16) == lane_head, q_rows, 0.0).astype(BF)
    def level(ref, half, l):
        return ref[half, PART * l:PART * (l + 1)]

    def spread(value, depth):
        return value[:PART * depth].reshape(depth, PART, value.shape[-1])

    def score_levels(half):
        for c in range(CHUNKS):
            at = slice(START[c], START[c] + SIZE[c])
            key = nn(xs[half, at], full[PK]).astype(BF)
            ps[half, at] = nt(key, qbt[...]) * SCALE
        top = level(ps, half, 0)
        for l in range(1, LEVELS):
            top = jnp.maximum(top, level(ps, half, l))
        norm = jnp.zeros_like(top)
        for l in range(LEVELS):
            e = jnp.exp(level(ps, half, l) - top)
            ps[half, PART * l:PART * (l + 1)] = e
            norm = norm + e
        inverse = 1.0 / norm
        for l in range(LEVELS):
            ps[half, PART * l:PART * (l + 1)] = level(ps, half, l) * inverse
        ps[half, PART * LEVELS:] = jnp.zeros((8, 128), F32)

    def project_values(half):
        for c in range(CHUNKS):
            at = slice(START[c], START[c] + SIZE[c])
            vs[half, at] = nn(xs[half, at], full[PV]).astype(BF)

    def mix(half):
        total = [jnp.zeros((PART, WIDTH), F32) for _ in range(3)]
        for c in range(CHUNKS):
            at = slice(START[c], START[c] + SIZE[c])
            value = vs[half, at].astype(F32)
            prob = ps[half, at].astype(BF)
            for a in range(3):
                total[a] = total[a] + jnp.sum(spread(nn(prob, ea[a]) * value, DEPTH[c]), axis=0)
        return jnp.concatenate(total + [jnp.zeros((8, WIDTH), F32)], axis=0).astype(BF)

    def latent_of(mixed):
        return (lq_row + nn(mixed, full[PO])).astype(BF)

    relay(PK)
    have(PK)
    score_levels(1)
    relay(PV)
    score_levels(0)
    have(PV)
    project_values(1)
    mixed = mix(1)
    relay(PO)
    have(PO)
    lat_l[...] = latent_of(mixed)
    send(remote(lat_l, lat_in, e_send.at[1], e_recv.at[1], (after, h)))
    relay(WO)
    project_values(0)
    latent = latent_of(mix(0))

    def normalise(at, value):
        z = value.astype(F32)
        z = z - jnp.mean(z, axis=-1, keepdims=True)
        inv = lax.rsqrt(jnp.mean(z * z, axis=-1, keepdims=True) + 1e-05)
        z = z * inv
        zs[at] = z
        inv_s[at] = jnp.broadcast_to(inv, (128, 128))
        return (z * gain_ref[...]).astype(BF)

    kept, lent = slice(0, 128), slice(128, 256)
    normed = normalise(kept, latent)
    relay(WQ)
    have(WO)
    remote(cot_l, cot_win.at[pl.ds(128, 128)], e_send.at[0], e_recv.at[0], (after, h)).wait_recv()
    win_o[...] = nt(cot_win[...], full[WO]).astype(BF)
    relay(WK)
    have(WQ)
    win_q[kept] = nn(normed, full[WQ]).astype(BF)
    relay(WV)
    have(WK)
    win_k[kept] = nn(normed, full[WK]).astype(BF)
    remote(lat_l, lat_in, e_send.at[1], e_recv.at[1], (after, h)).wait_recv()
    borrowed = normalise(lent, lat_in[...])
    win_q[lent] = nn(borrowed, full[WQ]).astype(BF)
    win_k[lent] = nn(borrowed, full[WK]).astype(BF)
    have(WV)
    win_v[kept] = nn(normed, full[WV]).astype(BF)
    win_v[lent] = nn(borrowed, full[WV]).astype(BF)

    def head_scores(i):
        lanes = slice(128 * (i // 4), 128 * (i // 4) + 128)
        mine = hot(lax.div(cols(128), 32) == i % 4)
        qm, om = win_q[:, lanes] * mine, win_o[:, lanes] * mine
        return qm, om, nt(win_k[:, lanes], qm), nt(win_v[:, lanes], om)

    state = {}

    def head_grads(i, prob, ds, qm, om):
        lanes = slice(128 * (i // 4), 128 * (i // 4) + 128)
        if i % 4 == 0:
            state["kt"] = win_k[:, lanes].astype(F32).T.astype(BF)
            state["gk"] = jnp.zeros((256, 128), F32)
            state["gv"] = jnp.zeros((256, 128), F32)
            state["gq"] = []
        state["gv"] = state["gv"] + nn(prob, om)
        state["gk"] = state["gk"] + nn(ds, qm)
        state["gq"].append(nn(state["kt"][32 * (i % 4):32 * (i % 4) + 32], ds))
        if i % 4 == 3:
            g_k[:, lanes] = state["gk"].astype(BF)
            g_v[:, lanes] = state["gv"].astype(BF)
            g_q[:, lanes] = jnp.concatenate(state["gq"], axis=0).T.astype(BF)

    following = head_scores(0)
    done = None
    for i in range(16):
        qm, om, score, dp = following
        if i < 15:
            following = head_scores(i + 1)
        if done is not None:
            head_grads(i - 1, *done)
        score = score * (SCALE * LOG2E) + bias[...]
        e = jnp.exp2(score - jnp.max(score, axis=0, keepdims=True))
        prob = e * (1.0 / jnp.sum(e, axis=0, keepdims=True))
        dp = dp - jnp.sum(prob * dp, axis=0, keepdims=True)
        done = (prob.astype(BF), (prob * dp * SCALE).astype(BF), qm, om)
    head_grads(15, *done)

    def shift_grad(at):
        d = nt(g_q[at], full[WQ]) + nt(g_k[at], full[WK]) + nt(g_v[at], full[WV])
        d = d * gain_ref[...]
        z = zs[at]
        return inv_s[at, 0:1] * (
            d - jnp.mean(d, axis=-1, keepdims=True) - z * jnp.mean(d * z, axis=-1, keepdims=True)
        )

    ds_l[...] = shift_grad(slice(128, 256)).astype(BF)
    send(remote(ds_l, ds_in, e_send.at[2], e_recv.at[2], (prev, h)))

    low_lanes = cols(128) < 64

    def own_part(half, c):
        lanes = pl.ds(pl.multiple_of(h * 128, 128), 128)
        at = pl.ds(144 * c, SENT[c])
        return pltpu.make_async_copy(ob.at[half, at, lanes], rv.at[h, half, at], own_sem.at[half, c])

    def backward(half, grad):
        d_mixed = nt(grad, full[PO]).astype(BF).astype(F32)
        d_mixed = [d_mixed[PART * a:PART * (a + 1)] for a in range(3)]
        for c in range(CHUNKS):
            size = PART * DEPTH[c]
            value = spread(vs[half, START[c]:START[c] + SIZE[c]].astype(F32), DEPTH[c])
            total = jnp.zeros((size, 128), F32)
            for a in range(3):
                prod = (value * d_mixed[a][None]).reshape(size, WIDTH)
                high = prod.astype(BF)
                low = (prod - high.astype(F32)).astype(BF)
                total = total + nt(high, ead[a]) + nt(low, ead[a])
            dps[START[c]:START[c] + size] = total
        mean = jnp.zeros((PART, 128), F32)
        for l in range(LEVELS):
            mean = mean + level(ps, half, l) * dps[PART * l:PART * (l + 1)]
        for c in range(CHUNKS):
            size = PART * DEPTH[c]
            prob = ps[half, START[c]:START[c] + size]
            dp = spread(dps[START[c]:START[c] + size], DEPTH[c])
            ds = prob * (dp - mean[None]).reshape(size, 128) * SCALE
            high = ds.astype(BF).astype(F32)
            ds = jnp.where(low_lanes, high, ds - high).astype(BF)
            grad_key = nn(ds, qbt[...]).astype(BF)
            prob = prob.astype(BF)
            grad_value = jnp.zeros((DEPTH[c], PART, WIDTH), F32)
            for a in range(3):
                grad_value = grad_value + d_mixed[a][None] * spread(nn(prob, ea[a]), DEPTH[c])
            grad_value = grad_value.reshape(size, WIDTH).astype(BF)
            total = (nt(grad_key, full[PK]) + nt(grad_value, full[PV])).astype(BF)
            total = nn(pack[...] if DEPTH[c] == 4 else pack1[...], total).astype(BF)
            ob[half, 144 * c:144 * c + SENT[c]] = total
            at = pl.ds(144 * c, SENT[c])
            for r, peer in ((1, over), (2, diag), (0, sib)):
                lanes = pl.ds(pl.multiple_of(peer * 128, 128), 128)
                send(remote(
                    ob.at[half, at, lanes], rv.at[h, half, at],
                    a_send.at[half, c, r], a_recv.at[half, c, r], (s, peer),
                ))
            own_part(half, c).start()

    grad = cot_win[0:128].astype(F32) + shift_grad(slice(0, 128))
    backward(0, grad.astype(BF))
    remote(ds_l, ds_in, e_send.at[2], e_recv.at[2], (prev, h)).wait_recv()
    grad = cot_l[...].astype(F32) + ds_in[...].astype(F32)
    backward(1, grad.astype(BF))

    for half in (0, 1):
        for c in range(CHUNKS):
            at = pl.ds(144 * c, SENT[c])
            for r, peer in enumerate((sib, over, diag)):
                place = rv.at[peer, half, at]
                remote(place, place, a_send.at[half, c, r], a_recv.at[half, c, r], (s, peer)).wait_recv()
            own_part(half, c).wait()
            parts = []
            for j in range(4):
                got = rv[j, half, 144 * c:144 * c + SENT[c]].astype(F32)
                parts.append(jnp.concatenate([got[:72], got[72:]], axis=1) if DEPTH[c] == 4 else got[:PART])
            got = jnp.concatenate(parts, axis=0).astype(BF)
            got = nn(unpack[...] if DEPTH[c] == 4 else unpack1[...], got).astype(BF)
            for i in range(DEPTH[c]):
                up, along = 144 * (i % 2), 128 * (i // 2)
                out[4 * c + i, 144 * half:144 * (half + 1)] = got[up:up + 144, along:along + 128]
    for copy in sent:
        copy.wait_send()


def per_device(levels, latent_query, w_pq, w_pk, w_pv, w_po, gain, wq, wk, wv, wo, cot):
    anywhere = pl.BlockSpec(memory_space=pl.ANY)
    scratch = [
        pltpu.VMEM((3, WIDTH), BF),
        pltpu.VMEM((WIDTH, 128), BF),
        pltpu.VMEM((1, WIDTH), F32),
        pltpu.VMEM((LEVELS, 6, 32, WIDTH), BF),
        pltpu.VMEM((3, 6, 32, WIDTH), BF),
        pltpu.VMEM((7, WIDTH, WIDTH), BF),
        pltpu.VMEM((16, WIDTH), F32),
        pltpu.VMEM((4, 16, 128), BF),
        pltpu.VMEM((128, WIDTH), BF),
        pltpu.VMEM((3, 128, WIDTH), BF),
        pltpu.VMEM((3, 128, WIDTH), BF),
        pltpu.VMEM((144, 160), BF),
        pltpu.VMEM((288, 288), BF),
        pltpu.VMEM((48, PART), BF),
        pltpu.VMEM((144, 160), BF),
        pltpu.VMEM((256, 256), F32),
        pltpu.VMEM((2, 528, WIDTH), BF),
        pltpu.VMEM((2, 528, WIDTH), BF),
        pltpu.VMEM((2, 528, 128), F32),
        pltpu.VMEM((528, 128), F32),
        pltpu.VMEM((128, WIDTH), BF),
        pltpu.VMEM((256, WIDTH), BF),
        pltpu.VMEM((128, WIDTH), BF),
        pltpu.VMEM((128, WIDTH), BF),
        pltpu.VMEM((128, WIDTH), BF),
        pltpu.VMEM((128, WIDTH), BF),
    ] + [pltpu.VMEM((256, WIDTH), BF) for _ in range(7)] + [
        pltpu.VMEM((256, WIDTH), F32),
        pltpu.VMEM((256, 128), F32),
        pltpu.VMEM((2, 480, WIDTH), BF),
        pltpu.VMEM((4, 2, 480, 128), BF),
    ] + [
        pltpu.SemaphoreType.DMA(shape)
        for shape in (
            (14,), (7, 5), (7, 5), (3,), (3,), (3,), (3,), (2, CHUNKS, 3), (2, CHUNKS, 3),
            (2, CHUNKS),
        )
    ]
    result = pl.pallas_call(
        kernel,
        out_shape=pltpu.VMEM((LEVELS, 288, 128), BF),
        in_specs=[anywhere] * 12,
        out_specs=pl.BlockSpec(memory_space=pltpu.VMEM),
        scratch_shapes=scratch,
        compiler_params=pltpu.CompilerParams(
            collective_id=0, has_side_effects=True, vmem_limit_bytes=VMEM_LIMIT
        ),
        name="encoder_backward",
    )(levels, latent_query, w_pq, w_pk, w_pv, w_po, gain.reshape(1, WIDTH), wq, wk, wv, wo, cot)
    return result.reshape(LEVELS, 6, 48, 128)


def solution(mesh):
    placed = (
        P(None, "space", None, None),
        P(),
        P(None, "head"),
        P(None, "head"),
        P(None, "head"),
        P("head", None),
        P(),
        P(None, "head"),
        P(None, "head"),
        P(None, "head"),
        P("head", None),
        P(None, "space", None, None),
    )
    return jax.shard_map(
        per_device,
        mesh=mesh,
        in_specs=placed,
        out_specs=P(None, "space", None, "head"),
        check_vma=False,
    )
```

```python
import functools

import jax
import jax.numpy as jnp
from jax import lax
from jax.experimental import pallas as pl
from jax.experimental.pallas import tpu as pltpu
from jax.sharding import PartitionSpec as P

X_CHIPS = 4
LEVELS = 13
CHUNKS = 4
WIDTH = 512
PART = 40
START = (0, 160, 320, 480)
SIZE = (160, 160, 160, 48)
DEPTH = (4, 4, 4, 1)
SENT = (144, 144, 144, 48)
VMEM_LIMIT = 60 * 1024 * 1024
SCALE = 32 ** (-0.5)
LOG2E = 1.4426950408889634
MESH = pl.DeviceIdType.MESH
BF = jnp.bfloat16
F32 = jnp.float32
PK, PV, PO, WO, WQ, WK, WV = range(7)
BY_COLUMN = (True, True, False, False, True, True, True)


def nn(left, right):
    return jnp.dot(left, right, preferred_element_type=F32)


def nt(left, right):
    return lax.dot_general(left, right, (((1,), (1,)), ((), ())), preferred_element_type=F32)


def rows(n):
    return lax.broadcasted_iota(jnp.int32, (n, 1), 0)


def cols(n):
    return lax.broadcasted_iota(jnp.int32, (1, n), 1)


def hot(condition):
    return jnp.where(condition, 1.0, 0.0).astype(BF)


def kernel(
    levels, lq_in, wpq_in, wpk, wpv, wpo, gain_in, wq, wk, wv, wo, cot,
    out,
    lq_ref, wpq_ref, gain_ref, lev, cotx, full, lqs, qbuf, qbt, ea, ead, pack, unpack, pack1, unpack1, bias,
    xs, vs, ps, dps, cot_l, cot_win, lat_l, lat_in, ds_l, ds_in,
    win_q, win_k, win_v, win_o, g_q, g_k, g_v, zs, inv_s, ob, rv,
    loc_sem, w_send, w_recv, q_send, q_recv, e_send, e_recv, a_send, a_recv, own_sem,
):
    s = lax.axis_index("space")
    n = lax.axis_size("space")
    h = lax.axis_index("head")
    sib = h + 1 - 2 * lax.rem(h, 2)
    over = lax.rem(h + 2, 4)
    diag = 3 - h
    z_other = s + X_CHIPS - 2 * X_CHIPS * lax.rem(lax.div(s, X_CHIPS), 2)
    prev = lax.rem(s + n - 1, n)
    after = lax.rem(s + 1, n)
    weights = (wpk, wpv, wpo, wo, wq, wk, wv)

    def region(k, head, part=None):
        if BY_COLUMN[k]:
            along = slice(None) if part is None else pl.ds(256 * part, 256)
            return full.at[k, along, pl.ds(pl.multiple_of(head * 128, 128), 128)]
        if part is None:
            return full.at[k, pl.ds(pl.multiple_of(head * 128, 128), 128)]
        return full.at[k, pl.ds(pl.multiple_of(head * 128 + 64 * part, 64), 64)]

    def shard(k, part):
        size = 256 if BY_COLUMN[k] else 64
        return weights[k].at[pl.ds(size * part, size)]

    def remote(src, dst, send, recv, device):
        return pltpu.make_async_remote_copy(
            src_ref=src, dst_ref=dst, send_sem=send, recv_sem=recv,
            device_id=device, device_id_type=MESH,
        )

    barrier = pltpu.get_barrier_semaphore()
    for device in (
        (s, sib), (s, over), (s, diag), (z_other, over), (prev, h), (after, h),
    ):
        pl.semaphore_signal(barrier, inc=1, device_id=device, device_id_type=MESH)

    b0 = lax.div(12 * h + 6, 16)
    b1 = lax.rem(b0 + 1, 3)
    base = 12 * h + 6 - 16 * b0
    local = []
    for block, where in ((b0, 0), (b1, 16)):
        at = pl.ds(pl.multiple_of(16 * block, 16), 16)
        local.append((levels.at[:, :, at, :], lev.at[pl.ds(0, LEVELS), :, pl.ds(where, 16), :]))
        local.append((cot.at[:, :, at, :], cotx.at[:, :, pl.ds(where, 16), :]))
    for k in range(7):
        local.append((weights[k], region(k, h)))
    for src, dst in ((lq_in, lq_ref), (wpq_in, wpq_ref), (gain_in, gain_ref)):
        local.append((src, dst))
    local = [
        pltpu.make_async_copy(src, dst, loc_sem.at[i]) for i, (src, dst) in enumerate(local)
    ]
    for copy in local[11:] + local[:11]:
        copy.start()

    local[11].wait()
    local[12].wait()
    local[13].wait()
    lqs[...] = jnp.zeros_like(lqs)
    lqs[0:3, :] = lq_ref[...].astype(F32)
    lq16 = lqs[...].astype(BF)
    qbuf[h] = nn(lq16, wpq_ref[...]).astype(BF)

    pl.semaphore_wait(barrier, 6)

    sent = []

    def send(copy):
        copy.start()
        sent.append(copy)

    def scatter(k):
        send(remote(shard(k, 0), region(k, h, 0), w_send.at[k, 1], w_recv.at[k, 1], (s, over)))
        send(remote(shard(k, 1), region(k, h, 1), w_send.at[k, 2], w_recv.at[k, 2], (z_other, over)))
        send(remote(weights[k], region(k, h), w_send.at[k, 0], w_recv.at[k, 0], (s, sib)))

    for r, peer in enumerate((sib, over, diag)):
        send(remote(qbuf.at[h], qbuf.at[h], q_send.at[r], q_recv.at[r], (s, peer)))
    for k in range(7):
        scatter(k)

    def wait_in(k, i, piece, device):
        remote(piece, piece, w_send.at[k, i], w_recv.at[k, i], device).wait_recv()

    def relay(k):
        for part, device in enumerate(((s, over), (z_other, over))):
            piece = region(k, over, part)
            wait_in(k, 1 + part, piece, device)
            send(remote(piece, piece, w_send.at[k, 3 + part], w_recv.at[k, 3 + part], (s, sib)))

    def have(k):
        local[4 + k].wait()
        wait_in(k, 0, region(k, sib), (s, sib))
        for part in range(2):
            wait_in(k, 3 + part, region(k, diag, part), (s, sib))

    lane_head = lax.div(cols(WIDTH), 32)
    for a in range(3):
        ea[a] = hot(rows(128) == a * 16 + lane_head)
        ead[a] = hot(lax.rem(rows(128), 64) == a * 16 + lane_head)
    k_row = lax.div(rows(144), 36) * PART + lax.rem(rows(144), 36)
    pack[...] = hot(k_row == cols(160))
    pack1[...] = hot(jnp.where(rows(48) < 36, rows(48), -1) == cols(PART))
    o_row = lax.rem(rows(288), 144)
    o_lon = lax.rem(lax.rem(o_row, 48) + 42, 48)
    o_cell = lax.div(o_row, 48) * 12 + lax.rem(o_lon, 12)
    unpack[...] = hot(lax.div(o_lon, 12) * 72 + lax.div(rows(288), 144) * 36 + o_cell == cols(288))
    unpack1[...] = hot((lax.div(o_lon, 12) * PART + o_cell)[:144] == cols(160))
    in_half = lax.rem(rows(256), 128)
    pad_key = jnp.logical_or(in_half >= 120, lax.rem(in_half, PART) >= 36)
    crossing = jnp.logical_and((rows(256) < 128) != (cols(256) < 128), s == 0)
    bias[...] = jnp.where(jnp.logical_or(pad_key, crossing), -1e30, 0.0).astype(F32)
    lq_row = nn(hot(lax.div(rows(128), PART) == cols(16)), lq16)

    local[0].wait()
    local[2].wait()
    cell = lax.rem(rows(80), PART)
    spot = lax.div(rows(80), PART) * 96 + lax.div(cell, 12) * 32 + base + lax.rem(cell, 12)
    take = hot(jnp.where(cell < 36, spot, -1) == cols(192))
    for c in range(CHUNKS):
        got = [nn(take, lev[4 * c + i].reshape(192, WIDTH)) for i in range(DEPTH[c])]
        for half in range(2):
            part = [one[PART * half:PART * (half + 1)] for one in got]
            if DEPTH[c] == 1:
                part.append(jnp.zeros((8, WIDTH), F32))
            xs[half, START[c]:START[c] + SIZE[c]] = jnp.concatenate(part, axis=0).astype(BF)

    local[1].wait()
    local[3].wait()
    cell = lax.rem(rows(128), PART)
    spot = lax.div(cell, 12) * 32 + base + lax.rem(cell, 12)
    spot = jnp.where(cell < 36, spot, -1000)
    for half in (1, 0):
        total = None
        for a in range(3):
            here = jnp.where(lax.div(rows(128), PART) == a, spot + half * 96, -1)
            term = nn(hot(here == cols(192)), cotx[a].reshape(192, WIDTH))
            total = term if total is None else total + term
        if half == 1:
            cot_l[...] = total.astype(BF)
            send(remote(cot_l, cot_win.at[pl.ds(128, 128)], e_send.at[0], e_recv.at[0], (after, h)))
        else:
            cot_win[0:128] = total.astype(BF)

    for r, peer in enumerate((sib, over, diag)):
        remote(qbuf.at[peer], qbuf.at[peer], q_send.at[r], q_recv.at[r], (s, peer)).wait_recv()
    q16 = jnp.concatenate([qbuf[i] for i in range(4)], axis=1)
    q_rows = nn(hot(lax.div(lax.rem(rows(128), 64), 16) == cols(16)), q16)
    qbt[...] = jnp.where(lax.rem(rows(128), 16) == lane_head, q_rows, 0.0).astype(BF)
    def level(ref, half, l):
        return ref[half, PART * l:PART * (l + 1)]

    def spread(value, depth):
        return value[:PART * depth].reshape(depth, PART, value.shape[-1])

    def score_levels(half):
        for c in range(CHUNKS):
            at = slice(START[c], START[c] + SIZE[c])
            key = nn(xs[half, at], full[PK]).astype(BF)
            ps[half, at] = nt(key, qbt[...]) * SCALE
        top = level(ps, half, 0)
        for l in range(1, LEVELS):
            top = jnp.maximum(top, level(ps, half, l))
        norm = jnp.zeros_like(top)
        for l in range(LEVELS):
            e = jnp.exp(level(ps, half, l) - top)
            ps[half, PART * l:PART * (l + 1)] = e
            norm = norm + e
        inverse = 1.0 / norm
        for l in range(LEVELS):
            ps[half, PART * l:PART * (l + 1)] = level(ps, half, l) * inverse
        ps[half, PART * LEVELS:] = jnp.zeros((8, 128), F32)

    def project_values(half):
        for c in range(CHUNKS):
            at = slice(START[c], START[c] + SIZE[c])
            vs[half, at] = nn(xs[half, at], full[PV]).astype(BF)

    def mix(half):
        total = [jnp.zeros((PART, WIDTH), F32) for _ in range(3)]
        for c in range(CHUNKS):
            at = slice(START[c], START[c] + SIZE[c])
            value = vs[half, at].astype(F32)
            prob = ps[half, at].astype(BF)
            for a in range(3):
                total[a] = total[a] + jnp.sum(spread(nn(prob, ea[a]) * value, DEPTH[c]), axis=0)
        return jnp.concatenate(total + [jnp.zeros((8, WIDTH), F32)], axis=0).astype(BF)

    def latent_of(mixed):
        return (lq_row + nn(mixed, full[PO])).astype(BF)

    relay(PK)
    have(PK)
    score_levels(1)
    relay(PV)
    score_levels(0)
    have(PV)
    relay(PO)
    project_values(1)
    mixed = mix(1)
    have(PO)
    lat_l[...] = latent_of(mixed)
    send(remote(lat_l, lat_in, e_send.at[1], e_recv.at[1], (after, h)))
    relay(WO)
    project_values(0)
    latent = latent_of(mix(0))

    def normalise(at, value):
        z = value.astype(F32)
        z = z - jnp.mean(z, axis=-1, keepdims=True)
        inv = lax.rsqrt(jnp.mean(z * z, axis=-1, keepdims=True) + 1e-05)
        z = z * inv
        zs[at] = z
        inv_s[at] = jnp.broadcast_to(inv, (128, 128))
        return (z * gain_ref[...]).astype(BF)

    kept, lent = slice(0, 128), slice(128, 256)
    normed = normalise(kept, latent)
    relay(WQ)
    have(WO)
    remote(cot_l, cot_win.at[pl.ds(128, 128)], e_send.at[0], e_recv.at[0], (after, h)).wait_recv()
    win_o[...] = nt(cot_win[...], full[WO]).astype(BF)
    relay(WK)
    have(WQ)
    win_q[kept] = nn(normed, full[WQ]).astype(BF)
    relay(WV)
    have(WK)
    win_k[kept] = nn(normed, full[WK]).astype(BF)
    remote(lat_l, lat_in, e_send.at[1], e_recv.at[1], (after, h)).wait_recv()
    borrowed = normalise(lent, lat_in[...])
    win_q[lent] = nn(borrowed, full[WQ]).astype(BF)
    win_k[lent] = nn(borrowed, full[WK]).astype(BF)
    have(WV)
    win_v[kept] = nn(normed, full[WV]).astype(BF)
    win_v[lent] = nn(borrowed, full[WV]).astype(BF)

    def head_scores(i):
        lanes = slice(128 * (i // 4), 128 * (i // 4) + 128)
        mine = hot(lax.div(cols(128), 32) == i % 4)
        qm, om = win_q[:, lanes] * mine, win_o[:, lanes] * mine
        return qm, om, nt(win_k[:, lanes], qm), nt(win_v[:, lanes], om)

    state = {}

    def head_grads(i, prob, ds, qm, om):
        lanes = slice(128 * (i // 4), 128 * (i // 4) + 128)
        if i % 4 == 0:
            state["kt"] = win_k[:, lanes].astype(F32).T.astype(BF)
            state["gk"] = jnp.zeros((256, 128), F32)
            state["gv"] = jnp.zeros((256, 128), F32)
            state["gq"] = []
        state["gv"] = state["gv"] + nn(prob, om)
        state["gk"] = state["gk"] + nn(ds, qm)
        state["gq"].append(nn(state["kt"][32 * (i % 4):32 * (i % 4) + 32], ds))
        if i % 4 == 3:
            g_k[:, lanes] = state["gk"].astype(BF)
            g_v[:, lanes] = state["gv"].astype(BF)
            g_q[:, lanes] = jnp.concatenate(state["gq"], axis=0).T.astype(BF)

    following = head_scores(0)
    done = None
    for i in range(16):
        qm, om, score, dp = following
        if i < 15:
            following = head_scores(i + 1)
        if done is not None:
            head_grads(i - 1, *done)
        score = score * (SCALE * LOG2E) + bias[...]
        e = jnp.exp2(score - jnp.max(score, axis=0, keepdims=True))
        prob = e * (1.0 / jnp.sum(e, axis=0, keepdims=True))
        dp = dp - jnp.sum(prob * dp, axis=0, keepdims=True)
        done = (prob.astype(BF), (prob * dp * SCALE).astype(BF), qm, om)
    head_grads(15, *done)

    def shift_grad(at):
        d = nt(g_q[at], full[WQ]) + nt(g_k[at], full[WK]) + nt(g_v[at], full[WV])
        d = d * gain_ref[...]
        z = zs[at]
        return inv_s[at, 0:1] * (
            d - jnp.mean(d, axis=-1, keepdims=True) - z * jnp.mean(d * z, axis=-1, keepdims=True)
        )

    shift = shift_grad(slice(0, 256))
    ds_l[...] = shift[128:].astype(BF)
    send(remote(ds_l, ds_in, e_send.at[2], e_recv.at[2], (prev, h)))

    low_lanes = cols(128) < 64

    def own_part(half, c):
        lanes = pl.ds(pl.multiple_of(h * 128, 128), 128)
        at = pl.ds(144 * c, SENT[c])
        return pltpu.make_async_copy(ob.at[half, at, lanes], rv.at[h, half, at], own_sem.at[half, c])

    def backward(half, grad):
        d_mixed = nt(grad, full[PO]).astype(BF).astype(F32)
        d_mixed = [d_mixed[PART * a:PART * (a + 1)] for a in range(3)]
        for c in range(CHUNKS):
            size = PART * DEPTH[c]
            value = spread(vs[half, START[c]:START[c] + SIZE[c]].astype(F32), DEPTH[c])
            total = jnp.zeros((size, 128), F32)
            for a in range(3):
                prod = (value * d_mixed[a][None]).reshape(size, WIDTH)
                high = prod.astype(BF)
                low = (prod - high.astype(F32)).astype(BF)
                total = total + nt(high, ead[a]) + nt(low, ead[a])
            dps[START[c]:START[c] + size] = total
        mean = jnp.zeros((PART, 128), F32)
        for l in range(LEVELS):
            mean = mean + level(ps, half, l) * dps[PART * l:PART * (l + 1)]
        for c in range(CHUNKS):
            size = PART * DEPTH[c]
            prob = ps[half, START[c]:START[c] + size]
            dp = spread(dps[START[c]:START[c] + size], DEPTH[c])
            ds = prob * (dp - mean[None]).reshape(size, 128) * SCALE
            high = ds.astype(BF).astype(F32)
            ds = jnp.where(low_lanes, high, ds - high).astype(BF)
            grad_key = nn(ds, qbt[...]).astype(BF)
            prob = prob.astype(BF)
            grad_value = jnp.zeros((DEPTH[c], PART, WIDTH), F32)
            for a in range(3):
                grad_value = grad_value + d_mixed[a][None] * spread(nn(prob, ea[a]), DEPTH[c])
            grad_value = grad_value.reshape(size, WIDTH).astype(BF)
            total = (nt(grad_key, full[PK]) + nt(grad_value, full[PV])).astype(BF)
            total = nn(pack[...] if DEPTH[c] == 4 else pack1[...], total).astype(BF)
            ob[half, 144 * c:144 * c + SENT[c]] = total
            at = pl.ds(144 * c, SENT[c])
            for r, peer in ((1, over), (2, diag), (0, sib)):
                lanes = pl.ds(pl.multiple_of(peer * 128, 128), 128)
                send(remote(
                    ob.at[half, at, lanes], rv.at[h, half, at],
                    a_send.at[half, c, r], a_recv.at[half, c, r], (s, peer),
                ))
            own_part(half, c).start()

    grad = cot_win[0:128].astype(F32) + shift[:128]
    backward(0, grad.astype(BF))
    remote(ds_l, ds_in, e_send.at[2], e_recv.at[2], (prev, h)).wait_recv()
    grad = cot_l[...].astype(F32) + ds_in[...].astype(F32)
    backward(1, grad.astype(BF))

    for half in (0, 1):
        for c in range(CHUNKS):
            at = pl.ds(144 * c, SENT[c])
            for r, peer in enumerate((sib, over, diag)):
                place = rv.at[peer, half, at]
                remote(place, place, a_send.at[half, c, r], a_recv.at[half, c, r], (s, peer)).wait_recv()
            own_part(half, c).wait()
            parts = []
            for j in range(4):
                got = rv[j, half, 144 * c:144 * c + SENT[c]].astype(F32)
                parts.append(jnp.concatenate([got[:72], got[72:]], axis=1) if DEPTH[c] == 4 else got[:PART])
            got = jnp.concatenate(parts, axis=0).astype(BF)
            got = nn(unpack[...] if DEPTH[c] == 4 else unpack1[...], got).astype(BF)
            for i in range(DEPTH[c]):
                up, along = 144 * (i % 2), 128 * (i // 2)
                out[4 * c + i, 144 * half:144 * (half + 1)] = got[up:up + 144, along:along + 128]
    for copy in sent:
        copy.wait_send()


def per_device(levels, latent_query, w_pq, w_pk, w_pv, w_po, gain, wq, wk, wv, wo, cot):
    anywhere = pl.BlockSpec(memory_space=pl.ANY)
    scratch = [
        pltpu.VMEM((3, WIDTH), BF),
        pltpu.VMEM((WIDTH, 128), BF),
        pltpu.VMEM((1, WIDTH), F32),
        pltpu.VMEM((LEVELS, 6, 32, WIDTH), BF),
        pltpu.VMEM((3, 6, 32, WIDTH), BF),
        pltpu.VMEM((7, WIDTH, WIDTH), BF),
        pltpu.VMEM((16, WIDTH), F32),
        pltpu.VMEM((4, 16, 128), BF),
        pltpu.VMEM((128, WIDTH), BF),
        pltpu.VMEM((3, 128, WIDTH), BF),
        pltpu.VMEM((3, 128, WIDTH), BF),
        pltpu.VMEM((144, 160), BF),
        pltpu.VMEM((288, 288), BF),
        pltpu.VMEM((48, PART), BF),
        pltpu.VMEM((144, 160), BF),
        pltpu.VMEM((256, 256), F32),
        pltpu.VMEM((2, 528, WIDTH), BF),
        pltpu.VMEM((2, 528, WIDTH), BF),
        pltpu.VMEM((2, 528, 128), F32),
        pltpu.VMEM((528, 128), F32),
        pltpu.VMEM((128, WIDTH), BF),
        pltpu.VMEM((256, WIDTH), BF),
        pltpu.VMEM((128, WIDTH), BF),
        pltpu.VMEM((128, WIDTH), BF),
        pltpu.VMEM((128, WIDTH), BF),
        pltpu.VMEM((128, WIDTH), BF),
    ] + [pltpu.VMEM((256, WIDTH), BF) for _ in range(7)] + [
        pltpu.VMEM((256, WIDTH), F32),
        pltpu.VMEM((256, 128), F32),
        pltpu.VMEM((2, 480, WIDTH), BF),
        pltpu.VMEM((4, 2, 480, 128), BF),
    ] + [
        pltpu.SemaphoreType.DMA(shape)
        for shape in (
            (14,), (7, 5), (7, 5), (3,), (3,), (3,), (3,), (2, CHUNKS, 3), (2, CHUNKS, 3),
            (2, CHUNKS),
        )
    ]
    result = pl.pallas_call(
        kernel,
        out_shape=pltpu.VMEM((LEVELS, 288, 128), BF),
        in_specs=[anywhere] * 12,
        out_specs=pl.BlockSpec(memory_space=pltpu.VMEM),
        scratch_shapes=scratch,
        compiler_params=pltpu.CompilerParams(
            collective_id=0, has_side_effects=True, vmem_limit_bytes=VMEM_LIMIT
        ),
        name="encoder_backward",
    )(levels, latent_query, w_pq, w_pk, w_pv, w_po, gain.reshape(1, WIDTH), wq, wk, wv, wo, cot)
    return result.reshape(LEVELS, 6, 48, 128)


def solution(mesh):
    placed = (
        P(None, "space", None, None),
        P(),
        P(None, "head"),
        P(None, "head"),
        P(None, "head"),
        P("head", None),
        P(),
        P(None, "head"),
        P(None, "head"),
        P(None, "head"),
        P("head", None),
        P(None, "space", None, None),
    )
    return jax.shard_map(
        per_device,
        mesh=mesh,
        in_specs=placed,
        out_specs=P(None, "space", None, "head"),
        check_vma=False,
    )
```

```python
import functools

import jax
import jax.numpy as jnp
from jax import lax
from jax.experimental import pallas as pl
from jax.experimental.pallas import tpu as pltpu
from jax.sharding import PartitionSpec as P

X_CHIPS = 4
LEVELS = 13
CHUNKS = 4
WIDTH = 512
PART = 40
START = (0, 160, 320, 480)
SIZE = (160, 160, 160, 48)
DEPTH = (4, 4, 4, 1)
SENT = (144, 144, 144, 48)
VMEM_LIMIT = 60 * 1024 * 1024
SCALE = 32 ** (-0.5)
LOG2E = 1.4426950408889634
MESH = pl.DeviceIdType.MESH
BF = jnp.bfloat16
F32 = jnp.float32
PK, PV, PO, WO, WQ, WK, WV = range(7)
BY_COLUMN = (True, True, False, False, True, True, True)


def nn(left, right):
    return jnp.dot(left, right, preferred_element_type=F32)


def nt(left, right):
    return lax.dot_general(left, right, (((1,), (1,)), ((), ())), preferred_element_type=F32)


def rows(n):
    return lax.broadcasted_iota(jnp.int32, (n, 1), 0)


def cols(n):
    return lax.broadcasted_iota(jnp.int32, (1, n), 1)


def hot(condition):
    return jnp.where(condition, 1.0, 0.0).astype(BF)


def kernel(
    levels, lq_in, wpq_in, wpk, wpv, wpo, gain_in, wq, wk, wv, wo, cot,
    out,
    lq_ref, wpq_ref, gain_ref, lev, cotx, full, lqs, qbuf, qbt, ea, ead, pack, unpack, pack1, unpack1, bias,
    xs, vs, ps, dps, cot_l, cot_win, lat_l, lat_in, ds_l, ds_in,
    win_q, win_k, win_v, win_o, g_q, g_k, g_v, zs, inv_s, ob, rv,
    loc_sem, w_send, w_recv, q_send, q_recv, e_send, e_recv, a_send, a_recv, own_sem,
):
    s = lax.axis_index("space")
    n = lax.axis_size("space")
    h = lax.axis_index("head")
    sib = h + 1 - 2 * lax.rem(h, 2)
    over = lax.rem(h + 2, 4)
    diag = 3 - h
    z_other = s + X_CHIPS - 2 * X_CHIPS * lax.rem(lax.div(s, X_CHIPS), 2)
    prev = lax.rem(s + n - 1, n)
    after = lax.rem(s + 1, n)
    weights = (wpk, wpv, wpo, wo, wq, wk, wv)

    def region(k, head, part=None):
        if BY_COLUMN[k]:
            along = slice(None) if part is None else pl.ds(256 * part, 256)
            return full.at[k, along, pl.ds(pl.multiple_of(head * 128, 128), 128)]
        if part is None:
            return full.at[k, pl.ds(pl.multiple_of(head * 128, 128), 128)]
        return full.at[k, pl.ds(pl.multiple_of(head * 128 + 64 * part, 64), 64)]

    def shard(k, part):
        size = 256 if BY_COLUMN[k] else 64
        return weights[k].at[pl.ds(size * part, size)]

    def remote(src, dst, send, recv, device):
        return pltpu.make_async_remote_copy(
            src_ref=src, dst_ref=dst, send_sem=send, recv_sem=recv,
            device_id=device, device_id_type=MESH,
        )

    barrier = pltpu.get_barrier_semaphore()
    for device in (
        (s, sib), (s, over), (s, diag), (z_other, over), (prev, h), (after, h),
    ):
        pl.semaphore_signal(barrier, inc=1, device_id=device, device_id_type=MESH)

    b0 = lax.div(12 * h + 6, 16)
    b1 = lax.rem(b0 + 1, 3)
    base = 12 * h + 6 - 16 * b0
    local = []
    for block, where in ((b0, 0), (b1, 16)):
        at = pl.ds(pl.multiple_of(16 * block, 16), 16)
        local.append((levels.at[:, :, at, :], lev.at[pl.ds(0, LEVELS), :, pl.ds(where, 16), :]))
        local.append((cot.at[:, :, at, :], cotx.at[:, :, pl.ds(where, 16), :]))
    for k in range(7):
        local.append((weights[k], region(k, h)))
    for src, dst in ((lq_in, lq_ref), (wpq_in, wpq_ref), (gain_in, gain_ref)):
        local.append((src, dst))
    local = [
        pltpu.make_async_copy(src, dst, loc_sem.at[i]) for i, (src, dst) in enumerate(local)
    ]
    for copy in local[11:] + local[1:4:2] + local[0:4:2] + local[4:11]:
        copy.start()

    local[11].wait()
    local[12].wait()
    local[13].wait()
    lqs[...] = jnp.zeros_like(lqs)
    lqs[0:3, :] = lq_ref[...].astype(F32)
    lq16 = lqs[...].astype(BF)
    qbuf[h] = nn(lq16, wpq_ref[...]).astype(BF)

    pl.semaphore_wait(barrier, 6)

    sent = []

    def send(copy):
        copy.start()
        sent.append(copy)

    def scatter(k):
        send(remote(shard(k, 0), region(k, h, 0), w_send.at[k, 1], w_recv.at[k, 1], (s, over)))
        send(remote(shard(k, 1), region(k, h, 1), w_send.at[k, 2], w_recv.at[k, 2], (z_other, over)))
        send(remote(weights[k], region(k, h), w_send.at[k, 0], w_recv.at[k, 0], (s, sib)))

    for r, peer in enumerate((sib, over, diag)):
        send(remote(qbuf.at[h], qbuf.at[h], q_send.at[r], q_recv.at[r], (s, peer)))
    for k in range(7):
        scatter(k)

    def wait_in(k, i, piece, device):
        remote(piece, piece, w_send.at[k, i], w_recv.at[k, i], device).wait_recv()

    def relay(k):
        for part, device in enumerate(((s, over), (z_other, over))):
            piece = region(k, over, part)
            wait_in(k, 1 + part, piece, device)
            send(remote(piece, piece, w_send.at[k, 3 + part], w_recv.at[k, 3 + part], (s, sib)))

    def have(k):
        local[4 + k].wait()
        wait_in(k, 0, region(k, sib), (s, sib))
        for part in range(2):
            wait_in(k, 3 + part, region(k, diag, part), (s, sib))

    lane_head = lax.div(cols(WIDTH), 32)
    for a in range(3):
        ea[a] = hot(rows(128) == a * 16 + lane_head)
        ead[a] = hot(lax.rem(rows(128), 64) == a * 16 + lane_head)
    k_row = lax.div(rows(144), 36) * PART + lax.rem(rows(144), 36)
    pack[...] = hot(k_row == cols(160))
    pack1[...] = hot(jnp.where(rows(48) < 36, rows(48), -1) == cols(PART))
    o_row = lax.rem(rows(288), 144)
    o_lon = lax.rem(lax.rem(o_row, 48) + 42, 48)
    o_cell = lax.div(o_row, 48) * 12 + lax.rem(o_lon, 12)
    unpack[...] = hot(lax.div(o_lon, 12) * 72 + lax.div(rows(288), 144) * 36 + o_cell == cols(288))
    unpack1[...] = hot((lax.div(o_lon, 12) * PART + o_cell)[:144] == cols(160))
    in_half = lax.rem(rows(256), 128)
    pad_key = jnp.logical_or(in_half >= 120, lax.rem(in_half, PART) >= 36)
    crossing = jnp.logical_and((rows(256) < 128) != (cols(256) < 128), s == 0)
    bias[...] = jnp.where(jnp.logical_or(pad_key, crossing), -1e30, 0.0).astype(F32)
    lq_row = nn(hot(lax.div(rows(128), PART) == cols(16)), lq16)

    local[1].wait()
    local[3].wait()
    cell = lax.rem(rows(128), PART)
    spot = lax.div(cell, 12) * 32 + base + lax.rem(cell, 12)
    spot = jnp.where(cell < 36, spot, -1000)
    for half in (1, 0):
        total = None
        for a in range(3):
            here = jnp.where(lax.div(rows(128), PART) == a, spot + half * 96, -1)
            term = nn(hot(here == cols(192)), cotx[a].reshape(192, WIDTH))
            total = term if total is None else total + term
        if half == 1:
            cot_l[...] = total.astype(BF)
            send(remote(cot_l, cot_win.at[pl.ds(128, 128)], e_send.at[0], e_recv.at[0], (after, h)))
        else:
            cot_win[0:128] = total.astype(BF)

    local[0].wait()
    local[2].wait()
    cell = lax.rem(rows(80), PART)
    spot = lax.div(rows(80), PART) * 96 + lax.div(cell, 12) * 32 + base + lax.rem(cell, 12)
    take = hot(jnp.where(cell < 36, spot, -1) == cols(192))
    for c in range(CHUNKS):
        got = [nn(take, lev[4 * c + i].reshape(192, WIDTH)) for i in range(DEPTH[c])]
        for half in range(2):
            part = [one[PART * half:PART * (half + 1)] for one in got]
            if DEPTH[c] == 1:
                part.append(jnp.zeros((8, WIDTH), F32))
            xs[half, START[c]:START[c] + SIZE[c]] = jnp.concatenate(part, axis=0).astype(BF)

    for r, peer in enumerate((sib, over, diag)):
        remote(qbuf.at[peer], qbuf.at[peer], q_send.at[r], q_recv.at[r], (s, peer)).wait_recv()
    q16 = jnp.concatenate([qbuf[i] for i in range(4)], axis=1)
    q_rows = nn(hot(lax.div(lax.rem(rows(128), 64), 16) == cols(16)), q16)
    qbt[...] = jnp.where(lax.rem(rows(128), 16) == lane_head, q_rows, 0.0).astype(BF)
    def level(ref, half, l):
        return ref[half, PART * l:PART * (l + 1)]

    def spread(value, depth):
        return value[:PART * depth].reshape(depth, PART, value.shape[-1])

    def score_levels(half):
        for c in range(CHUNKS):
            at = slice(START[c], START[c] + SIZE[c])
            key = nn(xs[half, at], full[PK]).astype(BF)
            ps[half, at] = nt(key, qbt[...]) * SCALE
        top = level(ps, half, 0)
        for l in range(1, LEVELS):
            top = jnp.maximum(top, level(ps, half, l))
        norm = jnp.zeros_like(top)
        for l in range(LEVELS):
            e = jnp.exp(level(ps, half, l) - top)
            ps[half, PART * l:PART * (l + 1)] = e
            norm = norm + e
        inverse = 1.0 / norm
        for l in range(LEVELS):
            ps[half, PART * l:PART * (l + 1)] = level(ps, half, l) * inverse
        ps[half, PART * LEVELS:] = jnp.zeros((8, 128), F32)

    def project_values(half):
        for c in range(CHUNKS):
            at = slice(START[c], START[c] + SIZE[c])
            vs[half, at] = nn(xs[half, at], full[PV]).astype(BF)

    def mix(half):
        total = [jnp.zeros((PART, WIDTH), F32) for _ in range(3)]
        for c in range(CHUNKS):
            at = slice(START[c], START[c] + SIZE[c])
            value = vs[half, at].astype(F32)
            prob = ps[half, at].astype(BF)
            for a in range(3):
                total[a] = total[a] + jnp.sum(spread(nn(prob, ea[a]) * value, DEPTH[c]), axis=0)
        return jnp.concatenate(total + [jnp.zeros((8, WIDTH), F32)], axis=0).astype(BF)

    def latent_of(mixed):
        return (lq_row + nn(mixed, full[PO])).astype(BF)

    relay(PK)
    have(PK)
    score_levels(1)
    relay(PV)
    score_levels(0)
    have(PV)
    relay(PO)
    project_values(1)
    mixed = mix(1)
    have(PO)
    lat_l[...] = latent_of(mixed)
    send(remote(lat_l, lat_in, e_send.at[1], e_recv.at[1], (after, h)))
    relay(WO)
    project_values(0)
    latent = latent_of(mix(0))

    def normalise(at, value):
        z = value.astype(F32)
        z = z - jnp.mean(z, axis=-1, keepdims=True)
        inv = lax.rsqrt(jnp.mean(z * z, axis=-1, keepdims=True) + 1e-05)
        z = z * inv
        zs[at] = z
        inv_s[at] = jnp.broadcast_to(inv, (128, 128))
        return (z * gain_ref[...]).astype(BF)

    kept, lent = slice(0, 128), slice(128, 256)
    normed = normalise(kept, latent)
    relay(WQ)
    have(WO)
    remote(cot_l, cot_win.at[pl.ds(128, 128)], e_send.at[0], e_recv.at[0], (after, h)).wait_recv()
    win_o[...] = nt(cot_win[...], full[WO]).astype(BF)
    relay(WK)
    have(WQ)
    win_q[kept] = nn(normed, full[WQ]).astype(BF)
    relay(WV)
    have(WK)
    win_k[kept] = nn(normed, full[WK]).astype(BF)
    remote(lat_l, lat_in, e_send.at[1], e_recv.at[1], (after, h)).wait_recv()
    borrowed = normalise(lent, lat_in[...])
    win_q[lent] = nn(borrowed, full[WQ]).astype(BF)
    win_k[lent] = nn(borrowed, full[WK]).astype(BF)
    have(WV)
    win_v[kept] = nn(normed, full[WV]).astype(BF)
    win_v[lent] = nn(borrowed, full[WV]).astype(BF)

    def head_scores(i):
        lanes = slice(128 * (i // 4), 128 * (i // 4) + 128)
        mine = hot(lax.div(cols(128), 32) == i % 4)
        qm, om = win_q[:, lanes] * mine, win_o[:, lanes] * mine
        return qm, om, nt(win_k[:, lanes], qm), nt(win_v[:, lanes], om)

    state = {}

    def head_grads(i, prob, ds, qm, om):
        lanes = slice(128 * (i // 4), 128 * (i // 4) + 128)
        if i % 4 == 0:
            state["kt"] = win_k[:, lanes].astype(F32).T.astype(BF)
            state["gk"] = jnp.zeros((256, 128), F32)
            state["gv"] = jnp.zeros((256, 128), F32)
            state["gq"] = []
        state["gv"] = state["gv"] + nn(prob, om)
        state["gk"] = state["gk"] + nn(ds, qm)
        state["gq"].append(nn(state["kt"][32 * (i % 4):32 * (i % 4) + 32], ds))
        if i % 4 == 3:
            g_k[:, lanes] = state["gk"].astype(BF)
            g_v[:, lanes] = state["gv"].astype(BF)
            g_q[:, lanes] = jnp.concatenate(state["gq"], axis=0).T.astype(BF)

    following = head_scores(0)
    done = None
    for i in range(16):
        qm, om, score, dp = following
        if i < 15:
            following = head_scores(i + 1)
        if done is not None:
            head_grads(i - 1, *done)
        score = score * (SCALE * LOG2E) + bias[...]
        e = jnp.exp2(score - jnp.max(score, axis=0, keepdims=True))
        prob = e * (1.0 / jnp.sum(e, axis=0, keepdims=True))
        dp = dp - jnp.sum(prob * dp, axis=0, keepdims=True)
        done = (prob.astype(BF), (prob * dp * SCALE).astype(BF), qm, om)
    head_grads(15, *done)

    def shift_grad(at):
        d = nt(g_q[at], full[WQ]) + nt(g_k[at], full[WK]) + nt(g_v[at], full[WV])
        d = d * gain_ref[...]
        z = zs[at]
        return inv_s[at, 0:1] * (
            d - jnp.mean(d, axis=-1, keepdims=True) - z * jnp.mean(d * z, axis=-1, keepdims=True)
        )

    shift = shift_grad(slice(0, 256))
    ds_l[...] = shift[128:].astype(BF)
    send(remote(ds_l, ds_in, e_send.at[2], e_recv.at[2], (prev, h)))

    low_lanes = cols(128) < 64

    def own_part(half, c):
        lanes = pl.ds(pl.multiple_of(h * 128, 128), 128)
        at = pl.ds(144 * c, SENT[c])
        return pltpu.make_async_copy(ob.at[half, at, lanes], rv.at[h, half, at], own_sem.at[half, c])

    def backward(half, grad):
        d_mixed = nt(grad, full[PO]).astype(BF).astype(F32)
        d_mixed = [d_mixed[PART * a:PART * (a + 1)] for a in range(3)]
        for c in range(CHUNKS):
            size = PART * DEPTH[c]
            value = spread(vs[half, START[c]:START[c] + SIZE[c]].astype(F32), DEPTH[c])
            total = jnp.zeros((size, 128), F32)
            for a in range(3):
                prod = (value * d_mixed[a][None]).reshape(size, WIDTH)
                high = prod.astype(BF)
                low = (prod - high.astype(F32)).astype(BF)
                total = total + nt(high, ead[a]) + nt(low, ead[a])
            dps[START[c]:START[c] + size] = total
        mean = jnp.zeros((PART, 128), F32)
        for l in range(LEVELS):
            mean = mean + level(ps, half, l) * dps[PART * l:PART * (l + 1)]
        for c in range(CHUNKS):
            size = PART * DEPTH[c]
            prob = ps[half, START[c]:START[c] + size]
            dp = spread(dps[START[c]:START[c] + size], DEPTH[c])
            ds = prob * (dp - mean[None]).reshape(size, 128) * SCALE
            high = ds.astype(BF).astype(F32)
            ds = jnp.where(low_lanes, high, ds - high).astype(BF)
            grad_key = nn(ds, qbt[...]).astype(BF)
            prob = prob.astype(BF)
            grad_value = jnp.zeros((DEPTH[c], PART, WIDTH), F32)
            for a in range(3):
                grad_value = grad_value + d_mixed[a][None] * spread(nn(prob, ea[a]), DEPTH[c])
            grad_value = grad_value.reshape(size, WIDTH).astype(BF)
            total = (nt(grad_key, full[PK]) + nt(grad_value, full[PV])).astype(BF)
            total = nn(pack[...] if DEPTH[c] == 4 else pack1[...], total).astype(BF)
            ob[half, 144 * c:144 * c + SENT[c]] = total
            at = pl.ds(144 * c, SENT[c])
            for r, peer in ((1, over), (2, diag), (0, sib)):
                lanes = pl.ds(pl.multiple_of(peer * 128, 128), 128)
                send(remote(
                    ob.at[half, at, lanes], rv.at[h, half, at],
                    a_send.at[half, c, r], a_recv.at[half, c, r], (s, peer),
                ))
            own_part(half, c).start()

    grad = cot_win[0:128].astype(F32) + shift[:128]
    backward(0, grad.astype(BF))
    remote(ds_l, ds_in, e_send.at[2], e_recv.at[2], (prev, h)).wait_recv()
    grad = cot_l[...].astype(F32) + ds_in[...].astype(F32)
    backward(1, grad.astype(BF))

    for half in (0, 1):
        for c in range(CHUNKS):
            at = pl.ds(144 * c, SENT[c])
            for r, peer in enumerate((sib, over, diag)):
                place = rv.at[peer, half, at]
                remote(place, place, a_send.at[half, c, r], a_recv.at[half, c, r], (s, peer)).wait_recv()
            own_part(half, c).wait()
            parts = []
            for j in range(4):
                got = rv[j, half, 144 * c:144 * c + SENT[c]].astype(F32)
                parts.append(jnp.concatenate([got[:72], got[72:]], axis=1) if DEPTH[c] == 4 else got[:PART])
            got = jnp.concatenate(parts, axis=0).astype(BF)
            got = nn(unpack[...] if DEPTH[c] == 4 else unpack1[...], got).astype(BF)
            for i in range(DEPTH[c]):
                up, along = 144 * (i % 2), 128 * (i // 2)
                out[4 * c + i, 144 * half:144 * (half + 1)] = got[up:up + 144, along:along + 128]
    for copy in sent:
        copy.wait_send()


def per_device(levels, latent_query, w_pq, w_pk, w_pv, w_po, gain, wq, wk, wv, wo, cot):
    anywhere = pl.BlockSpec(memory_space=pl.ANY)
    scratch = [
        pltpu.VMEM((3, WIDTH), BF),
        pltpu.VMEM((WIDTH, 128), BF),
        pltpu.VMEM((1, WIDTH), F32),
        pltpu.VMEM((LEVELS, 6, 32, WIDTH), BF),
        pltpu.VMEM((3, 6, 32, WIDTH), BF),
        pltpu.VMEM((7, WIDTH, WIDTH), BF),
        pltpu.VMEM((16, WIDTH), F32),
        pltpu.VMEM((4, 16, 128), BF),
        pltpu.VMEM((128, WIDTH), BF),
        pltpu.VMEM((3, 128, WIDTH), BF),
        pltpu.VMEM((3, 128, WIDTH), BF),
        pltpu.VMEM((144, 160), BF),
        pltpu.VMEM((288, 288), BF),
        pltpu.VMEM((48, PART), BF),
        pltpu.VMEM((144, 160), BF),
        pltpu.VMEM((256, 256), F32),
        pltpu.VMEM((2, 528, WIDTH), BF),
        pltpu.VMEM((2, 528, WIDTH), BF),
        pltpu.VMEM((2, 528, 128), F32),
        pltpu.VMEM((528, 128), F32),
        pltpu.VMEM((128, WIDTH), BF),
        pltpu.VMEM((256, WIDTH), BF),
        pltpu.VMEM((128, WIDTH), BF),
        pltpu.VMEM((128, WIDTH), BF),
        pltpu.VMEM((128, WIDTH), BF),
        pltpu.VMEM((128, WIDTH), BF),
    ] + [pltpu.VMEM((256, WIDTH), BF) for _ in range(7)] + [
        pltpu.VMEM((256, WIDTH), F32),
        pltpu.VMEM((256, 128), F32),
        pltpu.VMEM((2, 480, WIDTH), BF),
        pltpu.VMEM((4, 2, 480, 128), BF),
    ] + [
        pltpu.SemaphoreType.DMA(shape)
        for shape in (
            (14,), (7, 5), (7, 5), (3,), (3,), (3,), (3,), (2, CHUNKS, 3), (2, CHUNKS, 3),
            (2, CHUNKS),
        )
    ]
    result = pl.pallas_call(
        kernel,
        out_shape=pltpu.VMEM((LEVELS, 288, 128), BF),
        in_specs=[anywhere] * 12,
        out_specs=pl.BlockSpec(memory_space=pltpu.VMEM),
        scratch_shapes=scratch,
        compiler_params=pltpu.CompilerParams(
            collective_id=0, has_side_effects=True, vmem_limit_bytes=VMEM_LIMIT
        ),
        name="encoder_backward",
    )(levels, latent_query, w_pq, w_pk, w_pv, w_po, gain.reshape(1, WIDTH), wq, wk, wv, wo, cot)
    return result.reshape(LEVELS, 6, 48, 128)


def solution(mesh):
    placed = (
        P(None, "space", None, None),
        P(),
        P(None, "head"),
        P(None, "head"),
        P(None, "head"),
        P("head", None),
        P(),
        P(None, "head"),
        P(None, "head"),
        P(None, "head"),
        P("head", None),
        P(None, "space", None, None),
    )
    return jax.shard_map(
        per_device,
        mesh=mesh,
        in_specs=placed,
        out_specs=P(None, "space", None, "head"),
        check_vma=False,
    )
```
